32 devices in a mesh: wide: 8 (over y, x, core), narrow: 4 (over z).
Axes of the slice: x: 2, y: 2, z: 4, core: 2. Of those that a mesh axis runs over, the one named last changes fastest.
Arguments:
- images: bfloat16 [256, 24, 24, 384], P(('wide', 'narrow')), may hold values from -6 to 6
- cotangent: bfloat16 [256, 24, 24, 384], P(('wide', 'narrow')), may hold values from -6 to 6
- group_ids: int32 [256], P(('wide', 'narrow')), may hold values from 0 to 2
- keep_mask: int32 [256], P(('wide', 'narrow')), may hold values 0 or 1
- up_weight: float32 [384, 1536], P(None, ('wide', 'narrow')), may hold values from -0.3125 to 0.3125
- down_weight: float32 [1536, 384], P(('wide', 'narrow')), may hold values from -0.15625 to 0.15625
- small_params: float32 [22272], P(('wide', 'narrow')), may hold values from -1 to 1.5, as said below
- up_moment: float32 [384, 1536], P(None, ('wide', 'narrow')), may hold values from -64 to 64
- down_moment: float32 [1536, 384], P(('wide', 'narrow')), may hold values from -128 to 128
- small_moment: float32 [22272], P(('wide', 'narrow')), may hold values from -128 to 128
- up_second: float32 [384, 1536], P(None, ('wide', 'narrow')), may hold values from 10.10064 to 42.086
- down_second: float32 [1536, 384], P(('wide', 'narrow')), may hold values from 42.086 to 168.344
- small_second: float32 [22272], P(('wide', 'narrow')), may hold values from 30.30192 to 126.258
Outputs:
- activations: bfloat16 [256, 24, 24, 384], P(('wide', 'narrow'))
- input_grad: float32 [256, 24, 24, 384], P(('wide', 'narrow'))
- up_new: float32 [384, 1536], P(None, ('wide', 'narrow'))
- down_new: float32 [1536, 384], P(('wide', 'narrow'))
- small_new: float32 [22272], P(('wide', 'narrow'))
- up_first: float32 [384, 1536], P(None, ('wide', 'narrow'))
- down_first: float32 [1536, 384], P(('wide', 'narrow'))
- small_first: float32 [22272], P(('wide', 'narrow'))
- up_second_new: float32 [384, 1536], P(None, ('wide', 'narrow'))
- down_second_new: float32 [1536, 384], P(('wide', 'narrow'))
- small_second_new: float32 [22272], P(('wide', 'narrow'))
- up_copy: bfloat16 [384, 1536], P(None, ('wide', 'narrow'))
- down_copy: bfloat16 [1536, 384], P(('wide', 'narrow'))
- small_copy: bfloat16 [22272], P(('wide', 'narrow'))
The draws below stay inside these ranges and needn't reach their ends.
Inputs may be any that keep to these rules, and one draw needn't show every extreme that they name: `small_params`: rows 0 to 48 hold depthwise taps, row 50 the norm gain and row 53 the layer scale, both positive.
All inputs are finite; a program needn't handle non-finite values. No bound on the sum of `keep_mask` on one device may be relied on, other than what follows from the above.
Results may differ from the reference program's by a relative error of at most 0.0086.
Values may be sent and summed in bfloat16 or wider, within the bound.
A program may use at most 192 MiB of HBM per device.

```python
import math
import jax
import jax.numpy as jnp
from jax import lax

D = 384
H = 1536
SIDE_A = 14
SIDE_B = 18
SIDE_C = 24
STEP = 10
IMAGES = 256


def draw_small_params(key, part):
    key = jax.random.fold_in(key, 7)
    keys = jax.random.split(key, 5)
    taps = jax.random.truncated_normal(keys[0], -3.0, 3.0, (49, D), jnp.float32) / 7.0
    biases = 0.3 * jax.random.truncated_normal(keys[1], -3.0, 3.0, (3, D), jnp.float32)
    hidden_bias = 0.3 * jax.random.truncated_normal(keys[2], -3.0, 3.0, (4, D), jnp.float32)
    gains = jax.random.uniform(keys[3], (1, D), jnp.float32, 0.6, 1.4)
    scales = jax.random.uniform(keys[4], (1, D), jnp.float32, 0.5, 1.5)
    rows = jnp.concatenate([taps, biases[0:1], gains, biases[1:2], biases[2:3], scales, hidden_bias], axis=0)
    return rows.reshape(-1)


def place_ends(entries, stream_key, low, top_value):
    dims = entries.shape
    spot = [jax.random.randint(jax.random.fold_in(stream_key, axis), (), 0, dims[axis]) for axis in range(len(dims))]
    entries = entries.at[tuple(spot)].set(low)
    longest = dims.index(max(dims))
    spot[longest] = (spot[longest] + 1) % dims[longest]
    return entries.at[tuple(spot)].set(top_value)


def level_of(rng, dims, pieces, smallest, top_value):
    factor_of, own = 1.0, jax.random.fold_in(rng, 6)
    for axis_at, shards_of in pieces:
        heights = jnp.exp(jax.random.uniform(jax.random.fold_in(own, axis_at), (shards_of,), jnp.float32, smallest / len(pieces), top_value / len(pieces)))
        factor_of = factor_of * jnp.repeat(heights, dims[axis_at] // shards_of).reshape([-1 if axis == axis_at else 1 for axis in range(len(dims))])
    return factor_of


def noise(key, dims, deviation, bound, pieces=(), held_as=jnp.bfloat16):
    entries = jax.random.normal(key, dims, jnp.float32) * deviation
    if len(pieces) > 0:
        entries = level_of(key, dims, pieces, -0.22, 0.18) * entries
    return jnp.clip(entries, min=-bound, max=bound).astype(held_as)


def setup_inputs(seed: int = 0) -> dict:
    key_list = jax.random.split(jax.random.key(seed), 14)
    return {
        "images": noise(key_list[0], (IMAGES, SIDE_C, SIDE_C, D), 1.0, 6.0, ((0, 32),)),
        "cotangent": noise(key_list[1], (IMAGES, SIDE_C, SIDE_C, D), 1.0, 6.0, ((0, 32),)),
        "group_ids": place_ends(jax.random.randint(key_list[2], (IMAGES,), 0, 3), jax.random.fold_in(key_list[2], 1), 0, 2).astype(jnp.int32),
        "keep_mask": place_ends((jax.random.randint(key_list[3], (IMAGES,), 0, 10) < 9).astype(jnp.int32), jax.random.fold_in(key_list[3], 1), 0, 1),
        "up_weight": noise(key_list[4], (D, H), D ** -0.5, 0.3125, ((1, 32),), jnp.float32),
        "down_weight": noise(key_list[5], (H, D), H ** -0.5, 0.15625, ((0, 32),), jnp.float32),
        "small_params": draw_small_params(jax.random.fold_in(key_list[13], 71), 0),
        "up_moment": noise(key_list[7], (D, H), (0.04 * ((SIDE_A * SIDE_A + SIDE_B * SIDE_B + SIDE_C * SIDE_C) * IMAGES * 3 // 10) ** 0.5), 64.0, ((1, 32),), jnp.float32),
        "down_moment": noise(key_list[8], (H, D), (0.08 * ((SIDE_A * SIDE_A + SIDE_B * SIDE_B + SIDE_C * SIDE_C) * IMAGES * 3 // 10) ** 0.5), 128.0, ((0, 32),), jnp.float32),
        "small_moment": noise(key_list[9], (58 * D,), (0.07 * ((SIDE_A * SIDE_A + SIDE_B * SIDE_B + SIDE_C * SIDE_C) * IMAGES * 3 // 10) ** 0.5), 128.0, ((0, 32),), jnp.float32),
        "up_second": jnp.clip(jnp.exp(math.log(42.086) - 1.4271163 * jax.random.uniform(key_list[10], (D, H), jnp.float32) ** level_of(key_list[10], (D, H), ((1, 32),), -0.2, 0.2)), 10.10064, 42.086),
        "down_second": jnp.clip(jnp.exp(math.log(168.344) - 1.3862944 * jax.random.uniform(key_list[11], (H, D), jnp.float32) ** level_of(key_list[11], (H, D), ((0, 32),), -0.2, 0.2)), 42.086, 168.344),
        "small_second": jnp.clip(jnp.exp(math.log(126.258) - 1.4271164 * jax.random.uniform(key_list[12], (58 * D,), jnp.float32) ** level_of(key_list[12], (58 * D,), ((0, 32),), -0.2, 0.2)), 30.30192, 126.258),
    }


beta_one = 0.9
beta_two = 0.999
adam_eps = 1e-08
rate_mats = 0.02
rate_small = 0.05
decay_mats = 0.05

@jax.custom_vjp
def low(v):
    return lax.optimization_barrier(v.astype(jnp.bfloat16)).astype(jnp.float32)

@jax.custom_vjp
def low_back(v):
    return v

def low_keep(v):
    return (low(v), None)

def low_pass(kept, grad):
    return (grad,)

def back_keep(v):
    return (v, None)

def back_low(kept, grad):
    return (low(grad),)
low.defvjp(low_keep, low_pass)
low_back.defvjp(back_keep, back_low)

def side_of(group_ids):
    return jnp.where(group_ids == 0, SIDE_A, jnp.where(group_ids == 1, SIDE_B, SIDE_C)).astype(jnp.int32)

def valid_mask(sides):
    places = jnp.arange(SIDE_C, dtype=jnp.int32)
    inside = (places[None, :, None] < sides[:, None, None]) & (places[None, None, :] < sides[:, None, None])
    return inside.astype(jnp.float32)[..., None]

def forward(inputs, up_weight, down_weight, small_params, sides, drop):
    up_weight = low(up_weight)
    down_weight = low(down_weight)
    rows = low(small_params).reshape(58, D)
    taps = rows[:49]
    valid = valid_mask(sides)
    masked = inputs * valid
    padded = jnp.pad(masked, ((0, 0), (3, 3), (3, 3), (0, 0)))
    total = jnp.zeros_like(masked)
    for tap in range(49):
        row_off, col_off = divmod(tap, 7)
        total = total + taps[tap] * padded[:, row_off:row_off + SIDE_C, col_off:col_off + SIDE_C, :]
    conv = total + rows[49]
    center = conv - lax.optimization_barrier(jnp.mean(conv, axis=-1, keepdims=True))
    spread = lax.optimization_barrier(jnp.mean(center * center, axis=-1, keepdims=True))
    normed = center * lax.rsqrt(spread + 1e-06)
    act = low(normed * rows[50] + rows[51]).reshape(-1, D)
    pre = low_back(jnp.dot(act, up_weight, precision=lax.Precision.HIGHEST) + rows[54:].reshape(H))
    post = low(jax.nn.gelu(pre, approximate=False))
    proj = low_back(jnp.dot(post, down_weight, precision=lax.Precision.HIGHEST)).reshape(inputs.shape)
    branch = (proj + rows[52]) * rows[53] * drop[:, None, None, None]
    return valid * (inputs + branch)

def adam_update(weight, moment, second, grad, rate, decay):
    first = beta_one * moment + (1.0 - beta_one) * grad
    second_new = beta_two * second + (1.0 - beta_two) * grad * grad
    step_dir = first / (1.0 - beta_one ** STEP) / (jnp.sqrt(second_new / (1.0 - beta_two ** STEP)) + adam_eps)
    return (weight - rate * (step_dir + decay * weight), first, second_new)

def reference(images, cotangent, group_ids, keep_mask, up_weight, down_weight, small_params, up_moment, down_moment, small_moment, up_second, down_second, small_second):
    blocks = IMAGES // 8
    sides = side_of(group_ids).reshape(blocks, 8)
    drops = (keep_mask.astype(jnp.float32) / 0.9).reshape(blocks, 8)
    image_blocks = images.reshape(blocks, 8, SIDE_C, SIDE_C, D)
    cot_blocks = cotangent.reshape(blocks, 8, SIDE_C, SIDE_C, D)

    def one_block(carry, item):
        inputs, upstream, block_sides, block_drop = item

        def local(values, first_w, second_w, third_w):
            return forward(values, first_w, second_w, third_w, block_sides, block_drop)
        result, pull = jax.vjp(local, inputs.astype(jnp.float32), up_weight, down_weight, small_params)
        grads = pull(upstream.astype(jnp.float32))
        carry = (carry[0] + grads[1], carry[1] + grads[2], carry[2] + grads[3])
        return (carry, (result.astype(jnp.bfloat16), grads[0]))
    start = (jnp.zeros((D, H), jnp.float32), jnp.zeros((H, D), jnp.float32), jnp.zeros((58 * D,), jnp.float32))
    sums, outputs = lax.scan(one_block, start, (image_blocks, cot_blocks, sides, drops))
    activations = outputs[0].reshape(IMAGES, SIDE_C, SIDE_C, D)
    input_grad = outputs[1].reshape(IMAGES, SIDE_C, SIDE_C, D)
    up_new, up_first, up_second_new = adam_update(up_weight, up_moment, up_second, sums[0], rate_mats, decay_mats)
    down_new, down_first, down_second_new = adam_update(down_weight, down_moment, down_second, sums[1], rate_mats, decay_mats)
    small_new, small_first, small_second_new = adam_update(small_params, small_moment, small_second, sums[2], rate_small, 0.0)
    return (activations, input_grad, up_new, down_new, small_new, up_first, down_first, small_first, up_second_new, down_second_new, small_second_new, up_new.astype(jnp.bfloat16), down_new.astype(jnp.bfloat16), small_new.astype(jnp.bfloat16))
```

```python
from functools import partial

import jax
import jax.numpy as jnp
import ml_dtypes
import numpy as np
from jax import lax
from jax.experimental import pallas as pl
from jax.experimental.pallas import tpu as pltpu
from jax.sharding import PartitionSpec as P

SIDES = (14, 18, 24)
STEP = 10
BLOCK = 256
CHUNK = 256
VMEM_LIMIT = 60 * 1024 * 1024

beta_one = 0.9
beta_two = 0.999
adam_eps = 1e-08
rate_mats = 0.02
rate_small = 0.05
decay_mats = 0.05

BF = jnp.bfloat16
F32 = jnp.float32


def strips(total, step):
    return [(at, min(step, total - at)) for at in range(0, total, step)]


def round_up(value, step):
    return -(-value // step) * step


def make_tables(side, extent, rows):
    n = side + 3
    half = n // 2
    freqs = [(0, 0)] + [(0, v) for v in range(1, half + 1)]
    freqs += [(u, v) for u in range(1, half + 1) for v in range(n)]
    freqs = np.array(freqs, np.float64)
    count = len(freqs)
    compact = round_up(side * side, 16)
    wide = side * extent
    weight = (np.where(np.arange(count) == 0, 1.0, 2.0) / (n * n))[:, None]

    def angle(points):
        return 2.0 * np.pi / n * (freqs @ points.T)

    def stacked(top, bottom, offset):
        out = np.zeros((2 * offset, top.shape[1]), np.float64)
        out[:count] = top
        out[offset : offset + count] = bottom
        return out

    def widened(matrix, columns, spots):
        out = np.zeros((matrix.shape[0], columns), np.float64)
        out[:, spots] = matrix
        return out

    theta = angle(np.array([(i, j) for i in range(side) for j in range(side)], np.float64))
    shift = angle(np.array([(p - 3, q - 3) for p in range(7) for q in range(7)], np.float64))
    dense = np.arange(side * side)
    place = np.array([i * extent + j for i in range(side) for j in range(side)])
    own = round_up(count, 16)
    into = np.cos(theta), -np.sin(theta)
    back = weight * np.cos(theta), -weight * np.sin(theta)
    pick = np.zeros((compact, wide), np.float64)
    pick[dense, place] = 1.0
    return dict(
        freq=own,
        compact=compact,
        wide=wide,
        first_into=widened(stacked(*into, rows), extent * extent, place),
        first_back=np.pad(widened(stacked(*back, rows), compact, dense).T, ((0, extent * extent - compact), (0, 0))),
        first_taps=stacked(np.cos(shift), np.sin(shift), rows),
        into=widened(stacked(*into, own), compact, dense),
        back=widened(stacked(*back, own), wide, place).T,
        taps=np.pad(stacked(weight * np.cos(shift), -weight * np.sin(shift), own).T, ((0, 15), (0, 0))),
        pick=pick,
        spread=pick.T,
    )


def low_table(table):
    spare = round_up(table.shape[-1], 128) - table.shape[-1]
    return np.pad(table, ((0, 0),) * (table.ndim - 1) + ((0, spare),)).astype(ml_dtypes.bfloat16)


def split_table(table):
    high = table.astype(ml_dtypes.bfloat16)
    return low_table(high), low_table(table - high.astype(np.float64))


def stacked_split(table):
    pad = ((0, 0), (0, 0), (0, 64 - table.shape[2]))
    high = table.astype(ml_dtypes.bfloat16).astype(np.float64)
    return low_table(np.concatenate([np.pad(high, pad), np.pad(table - high, pad)], axis=2))


def spectrum_rows(extent):
    return round_up(((extent + 3) ** 2 + 1) // 2, 16)


def dot(left, right):
    return jnp.dot(left, right, preferred_element_type=F32)


def fold8(value):
    return jnp.sum(value.reshape(value.shape[0] // 8, 8, value.shape[1]), axis=0)


def twice_gelu(pre):
    part = pre * 0.7071067811865476
    level = 1.0 + lax.erf(part)
    bell = (pre * 0.7978845608028654) * jnp.exp2(part * part * -1.4426950408889634)
    return pre * level, level + bell


def dot_t(left, right):
    return lax.dot_general(left, right, (((1,), (1,)), ((), ())), preferred_element_type=F32)


def block_kernel(shapes, names, rows_f, extent, count, span, *refs):
    refs = list(refs)

    def take(number):
        got = refs[:number]
        del refs[:number]
        return got

    gid, keep = take(2)
    img_hbm, cot_hbm, act_far, normed_far, inv_far, spec_far, taps_far, up_far, down_far, rows = take(10)
    far_tables = [take(len(group)) for group in names]
    act_hbm, ig_hbm, up_out, down_out, small_out = take(5)
    img, cot, act_rows, normed_rows, inv_rows, cot_rows, spectra, taps_f = take(8)
    up_t, down, up_grad, down_grad, up_low, down_low = take(6)
    act_out, ig_out, work_a, work_b, prod = take(5)
    post_s, prg_s, act_t, pg_s, pg_t, eye, sums8, small = take(8)
    near_tables = [take(len(group)) for group in names]
    tables = [dict(zip(group, near)) for group, near in zip(names, near_tables)]
    cross = take(3)
    sem_img, sem_cot, sem_rows, sem_spec, sem_once, sem_out, sem_tables = take(7)

    images, pixels, width = img.shape
    hidden = up_t.shape[0]
    drop = float(np.float32(1.0) / np.float32(0.9))
    out_bias, scale, gain = rows[52:53, :], rows[53:54, :], rows[50:51, :]

    def group_of(b, s):
        if s == 0:
            return gid[b] == 0
        if s == 1:
            return gid[b] == 1
        return (gid[b] != 0) & (gid[b] != 1)

    def rows_of(b):
        sizes = [shape[1] for shape in shapes]
        size = jnp.where(gid[b] == 0, sizes[0], jnp.where(gid[b] == 1, sizes[1], sizes[2]))
        return jnp.where(keep[b] != 0, size, 0)

    def row_copies(b, off, compact):
        base = pl.multiple_of(off, 16)
        pairs = ((act_far, act_rows), (normed_far, normed_rows), (inv_far, inv_rows))
        return [
            pltpu.make_async_copy(
                far.at[b, pl.ds(0, compact)], near.at[pl.ds(base, compact)], sem_rows.at[k, b]
            )
            for k, (far, near) in enumerate(pairs)
        ]

    def cot_copy(b):
        return pltpu.make_async_copy(cot_hbm.at[b], cot.at[b], sem_cot.at[b])

    def img_copy(b):
        return pltpu.make_async_copy(img_hbm.at[b], img.at[b], sem_img.at[b])

    def spec_copy(b):
        return pltpu.make_async_copy(spec_far.at[b], spectra.at[b], sem_spec.at[b])

    mat_copies = [
        pltpu.make_async_copy(up_far, up_t, sem_once.at[0]),
        pltpu.make_async_copy(down_far, down, sem_once.at[1]),
    ]
    taps_copy = pltpu.make_async_copy(taps_far, taps_f, sem_once.at[2])
    grad_copies = [
        pltpu.make_async_copy(up_low, up_out, sem_once.at[3]),
        pltpu.make_async_copy(down_low, down_out, sem_once.at[4]),
    ]
    table_copies = []
    for s in range(3):
        for far, near in zip(far_tables[s], near_tables[s]):
            table_copies.append(
                pltpu.make_async_copy(far, near, sem_tables.at[len(table_copies)])
            )
    early = [k for k, name in enumerate(name for group in names for name in group) if name == "pick"]
    late = [k for k in range(len(table_copies)) if k not in early]

    for copy in mat_copies:
        copy.start()
    for k in early:
        table_copies[k].start()

    def fetch(b, off):
        cot_copy(b).start()
        for s in range(3):

            @pl.when((keep[b] != 0) & group_of(b, s))
            def _():
                for copy in row_copies(b, off, shapes[s][1]):
                    copy.start()

        return off + rows_of(b)

    total = lax.fori_loop(0, images, fetch, jnp.int32(0))
    up_grad[...] = jnp.zeros_like(up_grad)
    down_grad[...] = jnp.zeros_like(down_grad)
    first_row = lax.broadcasted_iota(jnp.int32, (16, BLOCK), 0) == 0
    act_t[width:, :] = jnp.where(first_row, 1.0, 0.0).astype(BF)
    same = lax.broadcasted_iota(jnp.int32, (CHUNK, CHUNK), 0) == lax.broadcasted_iota(
        jnp.int32, (CHUNK, CHUNK), 1
    )
    eye[...] = jnp.where(same, 1.0, 0.0).astype(BF)
    sums8[...] = jnp.zeros_like(sums8)
    for s in range(3):
        cross[s][...] = jnp.zeros_like(cross[s])
    end = pl.multiple_of(total, 16)
    act_rows[pl.ds(end, BLOCK), :] = jnp.zeros((BLOCK, width), BF)
    cot_rows[pl.ds(end, BLOCK), :] = jnp.zeros((BLOCK, width), BF)
    normed_rows[pl.ds(end, BLOCK), :] = jnp.zeros((BLOCK, width), BF)
    inv_rows[pl.ds(end, BLOCK), :] = jnp.zeros((BLOCK, 128), F32)
    for copy in mat_copies:
        copy.wait()
    for k in early:
        table_copies[k].wait()

    def middle(k, carry):
        base = pl.multiple_of(k * BLOCK, BLOCK)
        here = pl.ds(base, BLOCK)
        act = act_rows[here, :]
        act_t[0:width, :] = act.T
        pg_s[...] = (cot_rows[here, :].astype(F32) * (scale * drop)).astype(BF)
        pg_t[...] = pg_s[...].T
        for h in range(0, hidden, CHUNK):
            cols = slice(h, h + CHUNK)
            pre_all = dot_t(act, up_t[cols, :])
            back_all = dot_t(pg_s[...], down[cols, :])
            bias = small_bias(rows, h, CHUNK, width)
            for r, size in strips(BLOCK, 64):
                span = slice(r, r + size)
                post, slope = twice_gelu(pre_all[span] + bias)
                post_s[span, cols] = post.astype(BF)
                pull = back_all[span] * slope
                prg_s[span, cols] = pull.astype(BF)
        proj = dot(post_s[...], down[...])
        act_grad = dot(prg_s[...], up_t[...])
        for h in range(0, hidden, CHUNK):
            cols = slice(h, h + CHUNK)
            down_grad[:, cols] += dot(pg_t[...], post_s[:, cols])
            up_grad[:, cols] += dot(act_t[...], prg_s[:, cols])
        s_convb = sums8[0:8, :]
        s_gain = sums8[8:16, :]
        s_normb = sums8[16:24, :]
        s_cot = sums8[24:32, :]
        s_scale = sums8[32:40, :]
        for r, size in strips(BLOCK, 64):
            spot = pl.ds(base + r, size)
            shifted = proj[r : r + size] + 2.0 * out_bias
            arriving = cot_rows[spot, :].astype(F32)
            s_cot = s_cot + fold8(arriving)
            s_scale = s_scale + fold8(arriving * shifted)
            cot_rows[spot, :] = (shifted * (scale * (0.5 * drop))).astype(BF)
            grad = act_grad[r : r + size]
            normed = normed_rows[spot, :].astype(F32)
            s_gain = s_gain + fold8(grad * normed)
            s_normb = s_normb + fold8(grad)
            pulled = grad * (0.5 * gain)
            along = jnp.mean(pulled * normed, axis=1, keepdims=True)
            level = jnp.mean(pulled, axis=1, keepdims=True)
            inv = jnp.concatenate([inv_rows[spot, :]] * (width // 128), axis=1)
            conv_grad = inv * (pulled - level - normed * along)
            s_convb = s_convb + fold8(conv_grad)
            act_rows[spot, :] = conv_grad.astype(BF)
        sums8[0:8, :] = s_convb
        sums8[8:16, :] = s_gain
        sums8[16:24, :] = s_normb
        sums8[24:32, :] = s_cot
        sums8[32:40, :] = s_scale
        return carry

    def arrive(b, off):
        @pl.when(b < images)
        def _():
            cot_copy(b).wait()
            for s in range(3):
                _, compact, _, wide = shapes[s]

                @pl.when((keep[b] != 0) & group_of(b, s))
                def _():
                    base = pl.multiple_of(off, 16)
                    for copy in row_copies(b, off, compact):
                        copy.wait()
                    if wide < pixels:
                        cot_rows[pl.ds(base, compact), :] = dot(
                            tables[s]["pick"][:, 0:wide], cot[b, 0:wide, :]
                        ).astype(BF)
                    else:
                        cot_rows[pl.ds(base, compact), :] = cot[b]

            @pl.when(b == 1)
            def _():
                for k in late:
                    table_copies[k].start()
                taps_copy.start()
                for each in range(images):
                    spec_copy(each).start()
                    img_copy(each).start()

        inner = jnp.minimum(b, images - 1)
        after = off + jnp.where(b < images, rows_of(inner), BLOCK - 1)
        lax.fori_loop(off // BLOCK, after // BLOCK, middle, 0)
        return after

    lax.fori_loop(0, images + 1, arrive, jnp.int32(0))
    for h in range(0, hidden, CHUNK):
        cols = slice(h, h + CHUNK)
        up_low[cols, :] = dot_t(eye[...], (0.5 * up_grad[0:width, cols]).astype(BF)).astype(BF)
        down_low[cols, :] = dot_t(eye[...], (0.5 * down_grad[:, cols]).astype(BF)).astype(BF)
    for copy in grad_copies:
        copy.start()
    for k in late:
        table_copies[k].wait()
    taps_copy.wait()

    def out_copies(b, slot):
        return (
            pltpu.make_async_copy(act_out.at[slot], act_hbm.at[b], sem_out.at[0, slot]),
            pltpu.make_async_copy(ig_out.at[slot], ig_hbm.at[b], sem_out.at[1, slot]),
        )

    def last(b, off):
        slot = lax.rem(b, 2)
        img_copy(b).wait()
        spec_copy(b).wait()

        @pl.when(b >= 2)
        def _():
            for copy in out_copies(b - 2, slot):
                copy.wait()

        for s in range(3):
            side, compact, freq, wide = shapes[s]
            table = tables[s]
            inside = lax.broadcasted_iota(jnp.int32, (extent, width), 0) < side

            @pl.when((keep[b] != 0) & group_of(b, s))
            def _():
                base = pl.multiple_of(off, 16)
                work_a[0 : 2 * freq, :] = dot(
                    table["into"][:, 0:compact], act_rows[pl.ds(base, compact), :]
                )
                for r, size in strips(freq, 48):
                    lo, hi = slice(r, r + size), slice(freq + r, freq + r + size)
                    far = slice(rows_f + r, rows_f + r + size)
                    re, im = work_a[lo, :], work_a[hi, :]
                    x_re, x_im = spectra[b, lo, :].astype(F32), spectra[b, far, :].astype(F32)
                    cross[s][lo, :] += x_re * re + x_im * im
                    cross[s][hi, :] += x_im * re - x_re * im
                    t_re, t_im = taps_f[s, lo, :], taps_f[s, far, :]
                    prod[lo, :] = (re * t_re + im * t_im).astype(BF)
                    prod[hi, :] = (im * t_re - re * t_im).astype(BF)
                work_b[0:wide, :] = dot(table["back"][:, 0 : 2 * freq], prod[0 : 2 * freq, :])
                if wide < pixels:
                    work_a[0:wide, :] = dot(
                        table["spread"][:, 0:compact], cot_rows[pl.ds(base, compact), :]
                    )
                for r, size in strips(wide, extent if wide < pixels else 48):
                    spot = slice(r, r + size)
                    arriving = cot[b, spot, :].astype(F32)
                    value = img[b, spot, :].astype(F32)
                    if wide < pixels:
                        arriving = jnp.where(inside, arriving, 0.0)
                        value = jnp.where(inside, value, 0.0)
                        branch = work_a[spot, :]
                    else:
                        branch = cot_rows[pl.ds(base + r, size), :].astype(F32)
                    ig_out[slot, spot, :] = arriving + work_b[spot, :]
                    act_out[slot, spot, :] = (value + branch).astype(BF)

            @pl.when((keep[b] == 0) & group_of(b, s))
            def _():
                for i in range(side):
                    spot = slice(i * extent, (i + 1) * extent)
                    arriving = jnp.where(inside, cot[b, spot, :].astype(F32), 0.0)
                    ig_out[slot, spot, :] = arriving
                    value = jnp.where(inside, img[b, spot, :].astype(F32), 0.0)
                    act_out[slot, spot, :] = value.astype(BF)

            if wide < pixels:

                @pl.when(group_of(b, s))
                def _():
                    ig_out[slot, wide:, :] = jnp.zeros((pixels - wide, width), F32)
                    act_out[slot, wide:, :] = jnp.zeros((pixels - wide, width), BF)

        for copy in out_copies(b, slot):
            copy.start()
        return off + rows_of(b)

    lax.fori_loop(0, images, last, jnp.int32(0))

    taps_grad = jnp.zeros((64, width), F32)
    for s in range(3):
        freq = shapes[s][2]
        whole = cross[s][...]
        high = whole.astype(BF)
        rest = (whole - high.astype(F32)).astype(BF)
        taps_hi = tables[s]["taps_hi"][:, 0 : 2 * freq]
        taps_lo = tables[s]["taps_lo"][:, 0 : 2 * freq]
        taps_grad = taps_grad + dot(taps_hi, high) + dot(taps_lo, high) + dot(taps_hi, rest)
    small[...] = taps_grad

    def total8(at):
        return jnp.sum(sums8[at : at + 8, :], axis=0, keepdims=True)

    small[49:50, :] = total8(0)
    small[50:51, :] = total8(8) * 0.5
    small[51:52, :] = total8(16) * 0.5
    small[52:53, :] = total8(24) * (scale * drop)
    small[53:54, :] = total8(32) * (0.5 * drop)
    hid = 0.5 * up_grad[width : width + 1, :]
    for k in range(hidden // width):
        small[54 + k : 55 + k, :] = hid[:, k * width : (k + 1) * width]
    for d in range(small_out.shape[0]):
        row = d * count // width
        for k in range(span):
            small_out[d, :, k * width : (k + 1) * width] = small[row + k : row + k + 1, :]
    for copy in grad_copies:
        copy.wait()
    for b in range(max(images - 2, 0), images):
        for copy in out_copies(b, b % 2):
            copy.wait()


def small_bias(rows, start, count, width):
    parts = []
    while count > 0:
        row, col = divmod(start, width)
        size = min(count, width - col)
        parts.append(rows[54 + row : 55 + row, col : col + size])
        start, count = start + size, count - size
    return parts[0] if len(parts) == 1 else jnp.concatenate(parts, axis=1)


def run_block(images, cotangent, group_ids, keep_mask, first, up_t, down, devices, small_count):
    act, normed, inv, spectra, taps, rows = first
    count, extent, _, width = images.shape
    pixels = extent * extent
    hidden = up_t.shape[0]
    span = small_span(small_count, width)
    rows_f = spectrum_rows(extent)
    groups = [make_tables(side, extent, rows_f) for side in SIDES]
    shapes = [(side, g["compact"], g["freq"], g["wide"]) for side, g in zip(SIDES, groups)]
    names, flat = [], []
    for group in groups:
        tables = {"into": low_table(group["into"]), "back": low_table(group["back"])}
        tables["taps_hi"], tables["taps_lo"] = split_table(group["taps"])
        if group["wide"] < pixels:
            tables["pick"] = low_table(group["pick"])
            tables["spread"] = low_table(group["spread"])
        names.append(tuple(tables))
        flat += [jnp.asarray(table) for table in tables.values()]
    capacity = count * pixels + BLOCK
    vmem = pl.BlockSpec(memory_space=pltpu.VMEM)
    smem = pl.BlockSpec(memory_space=pltpu.SMEM)
    hbm = pl.BlockSpec(memory_space=pltpu.HBM)
    scratch = [
        pltpu.VMEM((count, pixels, width), BF),
        pltpu.VMEM((count, pixels, width), BF),
        pltpu.VMEM((capacity, width), BF),
        pltpu.VMEM((capacity, width), BF),
        pltpu.VMEM((capacity, 128), F32),
        pltpu.VMEM((capacity, width), BF),
        pltpu.VMEM(spectra.shape, BF),
        pltpu.VMEM(taps.shape, F32),
        pltpu.VMEM((hidden, width), BF),
        pltpu.VMEM((hidden, width), BF),
        pltpu.VMEM((width + 16, hidden), F32),
        pltpu.VMEM((width, hidden), F32),
        pltpu.VMEM((hidden, width), BF),
        pltpu.VMEM((hidden, width), BF),
        pltpu.VMEM((2, pixels, width), BF),
        pltpu.VMEM((2, pixels, width), F32),
        pltpu.VMEM((2 * rows_f, width), F32),
        pltpu.VMEM((pixels, width), F32),
        pltpu.VMEM((2 * rows_f, width), BF),
        pltpu.VMEM((BLOCK, hidden), BF),
        pltpu.VMEM((BLOCK, hidden), BF),
        pltpu.VMEM((width + 16, BLOCK), BF),
        pltpu.VMEM((BLOCK, width), BF),
        pltpu.VMEM((width, BLOCK), BF),
        pltpu.VMEM((CHUNK, CHUNK), BF),
        pltpu.VMEM((40, width), F32),
        pltpu.VMEM((64, width), F32),
    ]
    scratch += [pltpu.VMEM(table.shape, table.dtype) for table in flat]
    scratch += [pltpu.VMEM((2 * shape[2], width), F32) for shape in shapes]
    scratch += [
        pltpu.SemaphoreType.DMA((count,)),
        pltpu.SemaphoreType.DMA((count,)),
        pltpu.SemaphoreType.DMA((3, count)),
        pltpu.SemaphoreType.DMA((count,)),
        pltpu.SemaphoreType.DMA((5,)),
        pltpu.SemaphoreType.DMA((2, 2)),
        pltpu.SemaphoreType.DMA((len(flat),)),
    ]
    work = 6 * 2 * count * pixels * width * hidden
    return pl.pallas_call(
        partial(block_kernel, shapes, names, rows_f, extent, small_count, span),
        out_shape=(
            jax.ShapeDtypeStruct((count, pixels, width), BF),
            jax.ShapeDtypeStruct((count, pixels, width), F32),
            jax.ShapeDtypeStruct((hidden, width), BF),
            jax.ShapeDtypeStruct((hidden, width), BF),
            jax.ShapeDtypeStruct((devices, 1, span * width), F32),
        ),
        in_specs=[smem, smem] + [hbm] * 9 + [vmem] + [hbm] * len(flat),
        out_specs=(hbm, hbm, hbm, hbm, vmem),
        scratch_shapes=scratch,
        compiler_params=pltpu.CompilerParams(vmem_limit_bytes=VMEM_LIMIT),
        cost_estimate=pl.CostEstimate(flops=work, bytes_accessed=30000000, transcendentals=0),
        name="block",
    )(
        group_ids,
        keep_mask,
        images.reshape(count, pixels, width),
        cotangent.reshape(count, pixels, width),
        act,
        normed,
        inv,
        spectra,
        taps,
        up_t,
        down,
        rows,
        *flat,
    )


def adam_update(weight, moment, second, grad, rate, decay):
    first = beta_one * moment + (1.0 - beta_one) * grad
    second_new = beta_two * second + (1.0 - beta_two) * grad * grad
    step_dir = (
        first / (1.0 - beta_one**STEP) / (jnp.sqrt(second_new / (1.0 - beta_two**STEP)) + adam_eps)
    )
    return (weight - rate * (step_dir + decay * weight), first, second_new)


def wide_split(wide):
    chips = wide // 2
    high = 1
    while high * high < chips:
        high *= 2
    return high, chips // high


AXES = "hlcn"
GATHER_ROUTES = ("nhl", "lnh", "hln")
SCATTER_ROUTES = ("lhn", "hnl", "nlh")


class Place:
    def __init__(self, wide, narrow):
        high, low = wide_split(wide)
        self.sizes = dict(h=high, l=low, c=2, n=narrow)
        spot = lax.axis_index("wide")
        self.at = dict(
            h=spot // (2 * low),
            l=lax.rem(spot // 2, low),
            c=lax.rem(spot, 2),
            n=lax.axis_index("narrow"),
        )

    def shifted(self, axis, step):
        return lax.rem(self.at[axis] + step, self.sizes[axis])

    def device(self, axis, step):
        at = dict(self.at)
        at[axis] = self.shifted(axis, step)
        wide = (at["h"] * self.sizes["l"] + at["l"]) * 2 + at["c"]
        return {"wide": wide, "narrow": at["n"]}

    def peers(self):
        return [(axis, k) for axis in AXES for k in range(1, self.sizes[axis])]

    def greet(self):
        for axis, k in self.peers():
            pl.semaphore_signal(
                pltpu.get_barrier_semaphore(),
                inc=1,
                device_id=self.device(axis, k),
                device_id_type=pl.DeviceIdType.MESH,
            )

    def met(self):
        pl.semaphore_wait(pltpu.get_barrier_semaphore(), len(self.peers()))


def send(src, dst, sems, number, device):
    copy = pltpu.make_async_remote_copy(
        src_ref=src,
        dst_ref=dst,
        send_sem=sems[0].at[number],
        recv_sem=sems[1].at[number],
        device_id=device,
        device_id_type=pl.DeviceIdType.MESH,
    )
    copy.start()
    return copy


def make_parts(spaced, routes):
    tiles = spaced // 16
    cut = 16 * ((2 * tiles + 2) // 3)
    parts = [(2, (0, 1), routes[1]), (0, (0, spaced), routes[0]), (1, (0, cut), routes[1])]
    if cut < spaced:
        parts.append((1, (cut, spaced), routes[2]))
    return parts


def in_order(count, phases):
    return [(p, phase) for phase in range(phases) for p in range(count)]


def gather_copies(sizes):
    count = 1
    for axis in "hln":
        count += 2 * (sizes[axis] - 1)
    return count


def small_span(count, width):
    return (width + count - 2) // width + 1


def small_shift(wide, narrow, count, width):
    device = lax.axis_index("wide") * narrow + lax.axis_index("narrow")
    return lax.rem(device * count, width)


def gather_kernel(wide, narrow, parts, rows_f, *refs):
    refs = list(refs)

    def take(number):
        got = refs[:number]
        del refs[:number]
        return got

    gid = take(1)[0]
    far, img_hbm, far_tables = take(3), take(1)[0], take(3)
    up_hbm, down_hbm, rows, far_first = take(2) + [take(1)[0], take(5)]
    near, tables, bufs = take(3), take(3), take(3)
    img, xhat, act, normed, inv, spectra, taps_f = take(7)
    work, prod, rows_low, small_row = take(4)
    sem_in, sem_img, sem_tables, sem_first, sem_mats, send_sem, recv_sem = take(7)
    into, back, taps_in = tables
    place = Place(wide, narrow)
    here = tuple(place.at[axis] for axis in AXES)
    images, pixels, width = img.shape
    place.greet()
    fetch = [pltpu.make_async_copy(far[w], near[w], sem_in.at[w]) for w in range(3)]
    for copy in fetch:
        copy.start()
    fetch_tables = [
        pltpu.make_async_copy(far_tables[k], tables[k], sem_tables.at[k]) for k in range(3)
    ]

    def img_copy(b):
        return pltpu.make_async_copy(img_hbm.at[b], img.at[b], sem_img.at[b])

    for copy in fetch:
        copy.wait()
    fetch_tables[0].start()
    for b in range(images):
        img_copy(b).start()
    for copy in fetch_tables[1:]:
        copy.start()
    own, count = near[0].shape[0], near[2].shape[0]
    spaced = bufs[0].shape[4]
    for w in range(2):
        if own < spaced:
            bufs[w][here] = jnp.zeros(bufs[w].shape[4:], BF)
        bufs[w][here + (slice(0, own),)] = near[w][...].astype(BF)
    small_row[...] = jnp.zeros_like(small_row)
    small_row[:, 0:count] = near[2][...].reshape(1, count).astype(BF).astype(F32)
    bufs[2][here] = pltpu.roll(small_row[...], small_shift(wide, narrow, count, width), 1)
    place.met()
    sems = (send_sem, recv_sem)
    have = [dict(place.at) for _ in parts]
    started, sibling = [], []
    waiting = [None] * len(parts)
    passed = [[] for _ in parts]

    def region(p):
        which, bounds, _ = parts[p]
        return bufs[which].at[tuple(have[p][axis] for axis in AXES) + (slice(*bounds),)]

    def send_phase(p, phase):
        which, bounds, route = parts[p]
        axis = route[phase]
        waiting[p] = []
        for k in range(1, place.sizes[axis]):
            part = region(p)
            number = len(started) + len(sibling)
            waiting[p].append(send(part, part, sems, number, place.device(axis, k)))
            started.append(waiting[p][-1])

    def pass_over(p):
        number = len(started) + len(sibling)
        part = region(p)
        copy = send(part, part, sems, number, place.device("c", 1))
        sibling.append(copy)
        passed[p].append(copy)

    def finish_phase(p, phase):
        axis = parts[p][2][phase]
        for copy in waiting[p]:
            copy.wait_recv()
        before = have[p]
        have[p] = dict(before)
        have[p][axis] = slice(None)
        after = have[p]
        if phase < 2:
            send_phase(p, phase + 1)
        if phase == 0:
            pass_over(p)
        else:
            for k in range(1, place.sizes[axis]):
                have[p] = dict(before)
                have[p][axis] = place.shifted(axis, k)
                pass_over(p)
            have[p] = after

    def spectrum(b, carry):
        img_copy(b).wait()
        value = dot(into[gid[b], :, 0:pixels], img[b])
        xhat[b] = value
        spectra[b] = value.astype(BF)
        return carry

    def first_copies(b):
        pairs = zip((act, normed, inv, spectra), far_first)
        return [
            pltpu.make_async_copy(close.at[b], away.at[b], sem_first.at[k, b])
            for k, (close, away) in enumerate(pairs)
        ]

    def convolve(b, carry):
        g = gid[b]
        for r, size in strips(rows_f, 48):
            lo, hi = slice(r, r + size), slice(rows_f + r, rows_f + r + size)
            re, im = xhat[b, lo, :], xhat[b, hi, :]
            t_re, t_im = taps_f[g, lo, :], taps_f[g, hi, :]
            prod[lo, :] = (re * t_re - im * t_im).astype(BF)
            prod[hi, :] = (re * t_im + im * t_re).astype(BF)
        work[...] = dot(back[g, :, 0 : 2 * rows_f], prod[...])
        conv_bias, gain, norm_bias = rows[49:50, :], rows[50:51, :], rows[51:52, :]
        for r, size in strips(pixels, 64):
            span = slice(r, r + size)
            conv = work[span, :] + conv_bias
            center = conv - jnp.mean(conv, axis=1, keepdims=True)
            scale = lax.rsqrt(jnp.mean(center * center, axis=1, keepdims=True) + 1e-06)
            value = center * scale
            normed[b, span, :] = value.astype(BF)
            inv[b, span, :] = jnp.broadcast_to(scale, (size, 128))
            act[b, span, :] = (value * gain + norm_bias).astype(BF)
        for copy in first_copies(b):
            copy.start()
        return carry

    big = range(1, len(parts))
    ahead = max(images - 3, 0)
    for p in range(len(parts)):
        send_phase(p, 0)
    fetch_tables[0].wait()
    lax.fori_loop(0, images // 4, spectrum, 0)
    for p in range(len(parts)):
        finish_phase(p, 0)
    lax.fori_loop(images // 4, images // 2, spectrum, 0)
    finish_phase(0, 1)
    lax.fori_loop(images // 2, 3 * images // 4, spectrum, 0)
    finish_phase(0, 2)
    for p in big:
        finish_phase(p, 1)
    lax.fori_loop(3 * images // 4, images, spectrum, 0)
    for copy in fetch_tables[1:]:
        copy.wait()
    for copy in passed[0]:
        copy.wait_recv()
    collect_rows(bufs[2], count, rows)
    rows_low[0:64, :] = rows[...].astype(BF)
    rows_low[64:128, :] = rows[...].astype(BF)
    for s in range(3):
        taps_f[s] = dot(taps_in[s], rows_low[...])
    taps_copy = pltpu.make_async_copy(taps_f, far_first[4], sem_mats.at[2])
    taps_copy.start()
    lax.fori_loop(0, ahead, convolve, 0)
    for p in big:
        finish_phase(p, 2)
    lax.fori_loop(ahead, images - 1, convolve, 0)
    for p in big:
        for copy in passed[p]:
            copy.wait_recv()
    mats = [
        pltpu.make_async_copy(bufs[0], up_hbm, sem_mats.at[0]),
        pltpu.make_async_copy(bufs[1], down_hbm, sem_mats.at[1]),
    ]
    for copy in mats:
        copy.start()
    lax.fori_loop(images - 1, images, convolve, 0)

    def settle(b, carry):
        for copy in first_copies(b):
            copy.wait()
        return carry

    lax.fori_loop(0, images, settle, 0)
    for copy in mats:
        copy.wait()
    taps_copy.wait()
    for copy in started + sibling:
        copy.wait_send()


def collect_rows(pieces, count, rows):
    high, low, cores, narrow = pieces.shape[:4]
    width = rows.shape[1]
    terms = [[] for _ in range(rows.shape[0])]
    for d in range(high * low * cores * narrow):
        spot = (d // (low * cores * narrow), d // (cores * narrow) % low, d // narrow % cores, d % narrow)
        first, final = d * count // width, (d * count + count - 1) // width
        for r in range(first, final + 1):
            terms[r].append(pieces[spot][:, (r - first) * width : (r - first + 1) * width])
    for r, parts in enumerate(terms):
        value = jnp.zeros((1, width), F32)
        for part in parts:
            value = value + part
        rows[r : r + 1, :] = value


def gather_weights(wide, narrow, weights, images, group_ids):
    up, down, small = weights
    high, low = wide_split(wide)
    sizes = dict(h=high, l=low, n=narrow)
    own, width = up.shape
    images_n, extent = images.shape[:2]
    pixels = extent * extent
    count = small.shape[0]
    spaced = round_up(own, 16)
    lanes = small_span(count, width) * width
    grid = (high, low, 2, narrow)
    rows_f = spectrum_rows(extent)
    hbm = pl.BlockSpec(memory_space=pltpu.HBM)
    smem = pl.BlockSpec(memory_space=pltpu.SMEM)
    parts = make_parts(spaced, GATHER_ROUTES)
    copies = len(parts) * gather_copies(sizes)
    groups = [make_tables(side, extent, rows_f) for side in SIDES]
    tables = [
        low_table(np.stack([g["first_into"] for g in groups])),
        low_table(np.stack([g["first_back"] for g in groups])),
        stacked_split(np.stack([g["first_taps"] for g in groups])),
    ]
    first = [
        jax.ShapeDtypeStruct((images_n, pixels, width), BF),
        jax.ShapeDtypeStruct((images_n, pixels, width), BF),
        jax.ShapeDtypeStruct((images_n, pixels, 128), F32),
        jax.ShapeDtypeStruct((images_n, 2 * rows_f, width), BF),
        jax.ShapeDtypeStruct((3, 2 * rows_f, width), F32),
    ]
    bufs = [
        jax.ShapeDtypeStruct(grid + (spaced, width), BF),
        jax.ShapeDtypeStruct(grid + (spaced, width), BF),
        jax.ShapeDtypeStruct(grid + (1, lanes), F32),
    ]
    near = [
        pltpu.VMEM((own, width), F32),
        pltpu.VMEM((own, width), F32),
        pltpu.VMEM((count,), F32),
    ]
    scratch = near + [pltpu.VMEM(table.shape, BF) for table in tables]
    scratch += [pltpu.VMEM(buf.shape, buf.dtype) for buf in bufs]
    scratch += [
        pltpu.VMEM((images_n, pixels, width), BF),
        pltpu.VMEM((images_n, 2 * rows_f, width), F32),
    ]
    scratch += [pltpu.VMEM(part.shape, part.dtype) for part in first]
    scratch += [
        pltpu.VMEM((pixels, width), F32),
        pltpu.VMEM((2 * rows_f, width), BF),
        pltpu.VMEM((128, width), BF),
        pltpu.VMEM((1, lanes), F32),
        pltpu.SemaphoreType.DMA((3,)),
        pltpu.SemaphoreType.DMA((images_n,)),
        pltpu.SemaphoreType.DMA((4,)),
        pltpu.SemaphoreType.DMA((4, images_n)),
        pltpu.SemaphoreType.DMA((3,)),
        pltpu.SemaphoreType.DMA((copies,)),
        pltpu.SemaphoreType.DMA((copies,)),
    ]
    out = pl.pallas_call(
        partial(gather_kernel, wide, narrow, parts, rows_f),
        out_shape=tuple(bufs[:2] + [jax.ShapeDtypeStruct((64, width), F32)] + first),
        in_specs=[smem] + [hbm] * 7,
        out_specs=(hbm, hbm, pl.BlockSpec(memory_space=pltpu.VMEM)) + (hbm,) * 5,
        scratch_shapes=scratch,
        compiler_params=pltpu.CompilerParams(
            collective_id=0, has_side_effects=True, vmem_limit_bytes=VMEM_LIMIT
        ),
        name="gather",
    )(
        group_ids,
        up,
        down,
        small,
        images.reshape(images_n, pixels, width),
        *[jnp.asarray(table) for table in tables],
    )
    return out[0], out[1], out[3:] + (out[2],)


def scatter_shapes(sizes, parts, spaced, width, lanes):
    shapes = []
    for which, bounds, route in parts:
        tail, dtype = ((bounds[1] - bounds[0], width), BF) if which < 2 else ((1, lanes), F32)
        left = dict(h=sizes["h"], l=sizes["l"], n=sizes["n"])
        shapes.append(pltpu.VMEM(tuple(left.values()) + tail, dtype))
        for axis in route:
            del left[axis]
            shapes.append(
                pltpu.VMEM((max(sizes[axis] - 1, 1),) + tuple(left.values()) + tail, dtype)
            )
    return shapes


def scatter_kernel(wide, narrow, parts, *refs):
    refs = list(refs)

    def take(count):
        got = refs[:count]
        del refs[:count]
        return got

    far = take(3)
    sums_out = take(3)
    own, sums = take(3), take(3)
    landing = [take(4) for _ in parts]
    sem_own, send_sem, recv_sem = take(3)
    sems = (send_sem, recv_sem)
    place = Place(wide, narrow)
    place.greet()
    at, sizes = place.at, place.sizes
    full = slice(None)
    fetch = [
        pltpu.make_async_copy(far[w].at[full, full, at["c"]], own[w], sem_own.at[w])
        for w in range(3)
    ]
    for copy in fetch:
        copy.start()
    place.met()
    started = []
    for p, (which, bounds, route) in enumerate(parts):
        src = far[which].at[full, full, 1 - at["c"], full, slice(*bounds)]
        started.append(send(src, landing[p][0], sems, len(started), place.device("c", 1)))
    waiting = [[copy] for copy in started]
    left = [dict(h=full, l=full, n=full) for _ in parts]

    def spot(fixed):
        return tuple(fixed[axis] for axis in "hln")

    def send_phase(p, phase):
        which, bounds, route = parts[p]
        axis = route[phase]
        waiting[p] = []
        for k in range(1, sizes[axis]):
            there = dict(left[p])
            there[axis] = place.shifted(axis, k)
            src = sums[which].at[spot(there) + (slice(*bounds),)]
            dst = landing[p][1 + phase].at[k - 1]
            copy = send(src, dst, sems, len(started), place.device(axis, k))
            waiting[p].append(copy)
            started.append(copy)

    for copy in fetch:
        copy.wait()
    for p, phase in in_order(len(parts), 4):
        which, bounds, route = parts[p]
        rows = slice(*bounds)
        for copy in waiting[p]:
            copy.wait_recv()
        if phase == 0:
            for h in range(sizes["h"]):
                for l in range(sizes["l"]):
                    both = own[which][h, l, :, rows].astype(F32) + landing[p][0][h, l].astype(F32)
                    sums[which][h, l, :, rows] = both.astype(sums[which].dtype)
            send_phase(p, 0)
            continue
        axis = route[phase - 1]
        left[p][axis] = at[axis]
        target = spot(left[p]) + (rows,)
        total = sums[which][target].astype(F32)
        for k in range(1, sizes[axis]):
            total = total + landing[p][phase][k - 1].astype(F32)
        if phase < 3:
            sums[which][target] = total.astype(sums[which].dtype)
            send_phase(p, phase)
        else:
            sums_out[which][rows] = total
    for copy in started:
        copy.wait_send()


def scatter_sums(wide, narrow, partials):
    high, low = wide_split(wide)
    sizes = dict(h=high, l=low, n=narrow)
    spaced, width = partials[0].shape[4:]
    lanes = partials[2].shape[5]
    parts = make_parts(spaced, SCATTER_ROUTES)
    copies = len(parts) * (1 + sum(sizes[axis] - 1 for axis in "hln"))
    hbm = pl.BlockSpec(memory_space=pltpu.HBM)
    vmem = pl.BlockSpec(memory_space=pltpu.VMEM)
    grid = (high, low, narrow)
    halves = [
        pltpu.VMEM(grid + (spaced, width), BF),
        pltpu.VMEM(grid + (spaced, width), BF),
        pltpu.VMEM(grid + (1, lanes), F32),
    ]
    scratch = halves + halves + scatter_shapes(sizes, parts, spaced, width, lanes)
    scratch += [
        pltpu.SemaphoreType.DMA((3,)),
        pltpu.SemaphoreType.DMA((copies,)),
        pltpu.SemaphoreType.DMA((copies,)),
    ]
    return pl.pallas_call(
        partial(scatter_kernel, wide, narrow, parts),
        out_shape=(
            jax.ShapeDtypeStruct((spaced, width), F32),
            jax.ShapeDtypeStruct((spaced, width), F32),
            jax.ShapeDtypeStruct((1, lanes), F32),
        ),
        in_specs=[hbm] * 3,
        out_specs=(vmem,) * 3,
        scratch_shapes=scratch,
        compiler_params=pltpu.CompilerParams(
            collective_id=1, has_side_effects=True, vmem_limit_bytes=VMEM_LIMIT
        ),
        name="scatter",
    )(*partials)


def update_kernel(wide, narrow, width, *refs):
    grads, weights, moments, seconds = refs[0:3], refs[3:6], refs[6:9], refs[9:12]
    news, firsts, nexts, lows = refs[12:15], refs[15:18], refs[18:21], refs[21:24]
    for which in range(3):
        shape = weights[which].shape
        if which < 2:
            grad = grads[which][0 : shape[0], :]
        else:
            lanes = grads[which].shape[1]
            shift = lanes - small_shift(wide, narrow, shape[0], width)
            grad = pltpu.roll(grads[which][...], shift, 1)[:, 0 : shape[0]]

        def flat(value):
            return value if which < 2 else value.reshape(1, shape[0])

        rate, decay = (rate_mats, decay_mats) if which < 2 else (rate_small, 0.0)
        new, first, second = adam_update(
            flat(weights[which][...]),
            flat(moments[which][...]),
            flat(seconds[which][...]),
            grad,
            rate,
            decay,
        )
        news[which][...] = new.reshape(shape)
        firsts[which][...] = first.reshape(shape)
        nexts[which][...] = second.reshape(shape)
        lows[which][...] = new.reshape(shape).astype(BF)


def update(wide, narrow, grads, weights, moments, seconds):
    like = [jax.ShapeDtypeStruct(weight.shape, F32) for weight in weights]
    low = [jax.ShapeDtypeStruct(weight.shape, BF) for weight in weights]
    vmem = pl.BlockSpec(memory_space=pltpu.VMEM)
    return pl.pallas_call(
        partial(update_kernel, wide, narrow, weights[0].shape[1]),
        out_shape=tuple(like * 3 + low),
        in_specs=[vmem] * 12,
        out_specs=(vmem,) * 12,
        compiler_params=pltpu.CompilerParams(vmem_limit_bytes=VMEM_LIMIT),
        name="update",
    )(*grads, *weights, *moments, *seconds)


def per_device(
    wide,
    narrow,
    images,
    cotangent,
    group_ids,
    keep_mask,
    up_weight,
    down_weight,
    small_params,
    up_moment,
    down_moment,
    small_moment,
    up_second,
    down_second,
    small_second,
):
    width = images.shape[3]
    own, count = down_weight.shape[0], small_params.shape[0]
    devices = wide * narrow

    def laid(three):
        return three[0].T, three[1], three[2]

    weights = laid((up_weight, down_weight, small_params))
    moments = laid((up_moment, down_moment, small_moment))
    seconds = laid((up_second, down_second, small_second))
    gu, gd, first = gather_weights(wide, narrow, weights, images, group_ids)
    grid, spaced = gu.shape[:4], gu.shape[4]

    def dense(blocks):
        return blocks.reshape(devices, spaced, width)[:, :own].reshape(devices * own, width)

    def spread(rows):
        rows = rows.reshape(devices, own, width)
        return jnp.pad(rows, ((0, 0), (0, spaced - own), (0, 0))).reshape(
            grid + (spaced, width)
        )

    activations, input_grad, up_part, down_part, small_part = run_block(
        images, cotangent, group_ids, keep_mask, first, dense(gu), dense(gd), devices, count
    )
    small_part = small_part.reshape(grid + small_part.shape[1:])
    grads = scatter_sums(wide, narrow, (spread(up_part), spread(down_part), small_part))
    out = update(wide, narrow, grads, weights, moments, seconds)
    groups = [(out[k].T, out[k + 1], out[k + 2]) for k in range(0, 12, 3)]
    maps = (activations.reshape(images.shape), input_grad.reshape(images.shape))
    return maps + groups[0] + groups[1] + groups[2] + groups[3]


def solution(mesh):
    both = ("wide", "narrow")
    maps = P(both, None, None, None)
    cols, rows, flat = P(None, both), P(both, None), P(both)
    three = (cols, rows, flat)
    return jax.shard_map(
        partial(per_device, mesh.shape["wide"], mesh.shape["narrow"]),
        mesh=mesh,
        in_specs=(maps, maps, flat, flat) + three * 3,
        out_specs=(maps, maps) + three * 4,
        check_vma=False,
    )
```

```python
from functools import partial

import jax
import jax.numpy as jnp
import ml_dtypes
import numpy as np
from jax import lax
from jax.experimental import pallas as pl
from jax.experimental.pallas import tpu as pltpu
from jax.sharding import PartitionSpec as P

SIDES = (14, 18, 24)
STEP = 10
BLOCK = 256
CHUNK = 256
VMEM_LIMIT = 60 * 1024 * 1024

beta_one = 0.9
beta_two = 0.999
adam_eps = 1e-08
rate_mats = 0.02
rate_small = 0.05
decay_mats = 0.05

BF = jnp.bfloat16
F32 = jnp.float32


def strips(total, step):
    return [(at, min(step, total - at)) for at in range(0, total, step)]


def round_up(value, step):
    return -(-value // step) * step


def make_tables(side, extent, rows):
    n = side + 3
    half = n // 2
    freqs = [(0, 0)] + [(0, v) for v in range(1, half + 1)]
    freqs += [(u, v) for u in range(1, half + 1) for v in range(n)]
    freqs = np.array(freqs, np.float64)
    count = len(freqs)
    compact = round_up(side * side, 16)
    wide = side * extent
    weight = (np.where(np.arange(count) == 0, 1.0, 2.0) / (n * n))[:, None]

    def angle(points):
        return 2.0 * np.pi / n * (freqs @ points.T)

    def stacked(top, bottom, offset):
        out = np.zeros((2 * offset, top.shape[1]), np.float64)
        out[:count] = top
        out[offset : offset + count] = bottom
        return out

    def widened(matrix, columns, spots):
        out = np.zeros((matrix.shape[0], columns), np.float64)
        out[:, spots] = matrix
        return out

    theta = angle(np.array([(i, j) for i in range(side) for j in range(side)], np.float64))
    shift = angle(np.array([(p - 3, q - 3) for p in range(7) for q in range(7)], np.float64))
    dense = np.arange(side * side)
    place = np.array([i * extent + j for i in range(side) for j in range(side)])
    own = round_up(count, 16)
    into = np.cos(theta), -np.sin(theta)
    back = weight * np.cos(theta), -weight * np.sin(theta)
    pick = np.zeros((compact, wide), np.float64)
    pick[dense, place] = 1.0
    return dict(
        freq=own,
        compact=compact,
        wide=wide,
        first_into=widened(stacked(*into, rows), extent * extent, place),
        first_back=np.pad(widened(stacked(*back, rows), compact, dense).T, ((0, extent * extent - compact), (0, 0))),
        first_taps=stacked(np.cos(shift), np.sin(shift), rows),
        into=widened(stacked(*into, own), compact, dense),
        back=widened(stacked(*back, own), wide, place).T,
        taps=np.pad(stacked(weight * np.cos(shift), -weight * np.sin(shift), own).T, ((0, 15), (0, 0))),
        pick=pick,
        spread=pick.T,
    )


def low_table(table):
    spare = round_up(table.shape[-1], 128) - table.shape[-1]
    return np.pad(table, ((0, 0),) * (table.ndim - 1) + ((0, spare),)).astype(ml_dtypes.bfloat16)


def split_table(table):
    high = table.astype(ml_dtypes.bfloat16)
    return low_table(high), low_table(table - high.astype(np.float64))


def stacked_split(table):
    pad = ((0, 0), (0, 0), (0, 64 - table.shape[2]))
    high = table.astype(ml_dtypes.bfloat16).astype(np.float64)
    return low_table(np.concatenate([np.pad(high, pad), np.pad(table - high, pad)], axis=2))


def spectrum_rows(extent):
    return round_up(((extent + 3) ** 2 + 1) // 2, 16)


def dot(left, right):
    return jnp.dot(left, right, preferred_element_type=F32)


def fold8(value):
    return jnp.sum(value.reshape(value.shape[0] // 8, 8, value.shape[1]), axis=0)


def twice_gelu(pre):
    part = pre * 0.7071067811865476
    level = 1.0 + lax.erf(part)
    bell = (pre * 0.7978845608028654) * jnp.exp(-(part * part))
    return pre * level, level + bell


def dot_t(left, right):
    return lax.dot_general(left, right, (((1,), (1,)), ((), ())), preferred_element_type=F32)


def block_kernel(shapes, names, rows_f, extent, count, span, *refs):
    refs = list(refs)

    def take(number):
        got = refs[:number]
        del refs[:number]
        return got

    gid, keep = take(2)
    img_hbm, cot_hbm, act_far, normed_far, inv_far, spec_far, taps_far, up_far, down_far, rows = take(10)
    far_tables = [take(len(group)) for group in names]
    act_hbm, ig_hbm, up_out, down_out, small_out = take(5)
    img, cot, act_rows, normed_rows, inv_rows, cot_rows, spectra, taps_f = take(8)
    up_t, down, up_c, down_c, up_grad, down_grad, up_low, down_low = take(8)
    act_out, ig_out, work_a, work_b, prod = take(5)
    post_s, prg_s, act_t, pg_s, pg_t, eye, sums8, small = take(8)
    near_tables = [take(len(group)) for group in names]
    tables = [dict(zip(group, near)) for group, near in zip(names, near_tables)]
    cross = take(3)
    sem_img, sem_cot, sem_rows, sem_spec, sem_once, sem_out, sem_tables = take(7)

    images, pixels, width = img.shape
    hidden = up_t.shape[0]
    drop = float(np.float32(1.0) / np.float32(0.9))
    out_bias, scale, gain = rows[52:53, :], rows[53:54, :], rows[50:51, :]

    def group_of(b, s):
        if s == 0:
            return gid[b] == 0
        if s == 1:
            return gid[b] == 1
        return (gid[b] != 0) & (gid[b] != 1)

    def rows_of(b):
        sizes = [shape[1] for shape in shapes]
        size = jnp.where(gid[b] == 0, sizes[0], jnp.where(gid[b] == 1, sizes[1], sizes[2]))
        return jnp.where(keep[b] != 0, size, 0)

    def row_copies(b, off, compact):
        base = pl.multiple_of(off, 16)
        pairs = ((act_far, act_rows), (normed_far, normed_rows), (inv_far, inv_rows))
        return [
            pltpu.make_async_copy(
                far.at[b, pl.ds(0, compact)], near.at[pl.ds(base, compact)], sem_rows.at[k, b]
            )
            for k, (far, near) in enumerate(pairs)
        ]

    def cot_copy(b):
        return pltpu.make_async_copy(cot_hbm.at[b], cot.at[b], sem_cot.at[b])

    def img_copy(b):
        return pltpu.make_async_copy(img_hbm.at[b], img.at[b], sem_img.at[b])

    def spec_copy(b):
        return pltpu.make_async_copy(spec_far.at[b], spectra.at[b], sem_spec.at[b])

    mat_copies = [
        pltpu.make_async_copy(up_far, up_t, sem_once.at[0]),
        pltpu.make_async_copy(down_far, down, sem_once.at[1]),
    ]
    taps_copy = pltpu.make_async_copy(taps_far, taps_f, sem_once.at[2])
    grad_copies = [
        pltpu.make_async_copy(up_low, up_out, sem_once.at[3]),
        pltpu.make_async_copy(down_low, down_out, sem_once.at[4]),
    ]
    table_copies = []
    for s in range(3):
        for far, near in zip(far_tables[s], near_tables[s]):
            table_copies.append(
                pltpu.make_async_copy(far, near, sem_tables.at[len(table_copies)])
            )
    early = [k for k, name in enumerate(name for group in names for name in group) if name == "pick"]
    late = [k for k in range(len(table_copies)) if k not in early]

    for copy in mat_copies:
        copy.start()
    for k in early:
        table_copies[k].start()

    def fetch(b, off):
        cot_copy(b).start()
        for s in range(3):

            @pl.when((keep[b] != 0) & group_of(b, s))
            def _():
                for copy in row_copies(b, off, shapes[s][1]):
                    copy.start()

        return off + rows_of(b)

    total = lax.fori_loop(0, images, fetch, jnp.int32(0))
    up_grad[...] = jnp.zeros_like(up_grad)
    down_grad[...] = jnp.zeros_like(down_grad)
    first_row = lax.broadcasted_iota(jnp.int32, (16, BLOCK), 0) == 0
    act_t[width:, :] = jnp.where(first_row, 1.0, 0.0).astype(BF)
    same = lax.broadcasted_iota(jnp.int32, (CHUNK, CHUNK), 0) == lax.broadcasted_iota(
        jnp.int32, (CHUNK, CHUNK), 1
    )
    eye[...] = jnp.where(same, 1.0, 0.0).astype(BF)
    sums8[...] = jnp.zeros_like(sums8)
    for s in range(3):
        cross[s][...] = jnp.zeros_like(cross[s])
    end = pl.multiple_of(total, 16)
    act_rows[pl.ds(end, BLOCK), :] = jnp.zeros((BLOCK, width), BF)
    cot_rows[pl.ds(end, BLOCK), :] = jnp.zeros((BLOCK, width), BF)
    normed_rows[pl.ds(end, BLOCK), :] = jnp.zeros((BLOCK, width), BF)
    inv_rows[pl.ds(end, BLOCK), :] = jnp.zeros((BLOCK, 128), F32)
    for copy in mat_copies:
        copy.wait()
    for h in range(0, hidden, CHUNK):
        cols = slice(h, h + CHUNK)
        up_c[:, cols] = up_t[cols, :].T
        down_c[:, cols] = down[cols, :].T
    for k in early:
        table_copies[k].wait()

    def middle(k, carry):
        base = pl.multiple_of(k * BLOCK, BLOCK)
        here = pl.ds(base, BLOCK)
        act = act_rows[here, :]
        act_t[0:width, :] = act.T
        pg_s[...] = (cot_rows[here, :].astype(F32) * (scale * drop)).astype(BF)
        pg_t[...] = pg_s[...].T
        for h in range(0, hidden, CHUNK):
            cols = slice(h, h + CHUNK)
            pre_all = dot_t(act, up_t[cols, :])
            back_all = dot_t(pg_s[...], down[cols, :])
            bias = small_bias(rows, h, CHUNK, width)
            for r, size in strips(BLOCK, 64):
                span = slice(r, r + size)
                post, slope = twice_gelu(pre_all[span] + bias)
                post_s[span, cols] = post.astype(BF)
                pull = back_all[span] * slope
                prg_s[span, cols] = pull.astype(BF)
        proj = dot_t(down_c[...], post_s[...]).T
        act_grad = dot_t(up_c[...], prg_s[...]).T
        for h in range(0, hidden, CHUNK):
            cols = slice(h, h + CHUNK)
            down_grad[:, cols] += dot(pg_t[...], post_s[:, cols])
            up_grad[:, cols] += dot(act_t[...], prg_s[:, cols])
        s_convb = sums8[0:8, :]
        s_gain = sums8[8:16, :]
        s_normb = sums8[16:24, :]
        s_cot = sums8[24:32, :]
        s_scale = sums8[32:40, :]
        for r, size in strips(BLOCK, 64):
            spot = pl.ds(base + r, size)
            shifted = proj[r : r + size] + 2.0 * out_bias
            arriving = cot_rows[spot, :].astype(F32)
            s_cot = s_cot + fold8(arriving)
            s_scale = s_scale + fold8(arriving * shifted)
            cot_rows[spot, :] = (shifted * (scale * (0.5 * drop))).astype(BF)
            grad = act_grad[r : r + size]
            normed = normed_rows[spot, :].astype(F32)
            s_gain = s_gain + fold8(grad * normed)
            s_normb = s_normb + fold8(grad)
            pulled = grad * (0.5 * gain)
            along = jnp.mean(pulled * normed, axis=1, keepdims=True)
            level = jnp.mean(pulled, axis=1, keepdims=True)
            inv = jnp.concatenate([inv_rows[spot, :]] * (width // 128), axis=1)
            conv_grad = inv * (pulled - level - normed * along)
            s_convb = s_convb + fold8(conv_grad)
            act_rows[spot, :] = conv_grad.astype(BF)
        sums8[0:8, :] = s_convb
        sums8[8:16, :] = s_gain
        sums8[16:24, :] = s_normb
        sums8[24:32, :] = s_cot
        sums8[32:40, :] = s_scale
        return carry

    def arrive(b, off):
        @pl.when(b < images)
        def _():
            cot_copy(b).wait()
            for s in range(3):
                _, compact, _, wide = shapes[s]

                @pl.when((keep[b] != 0) & group_of(b, s))
                def _():
                    base = pl.multiple_of(off, 16)
                    for copy in row_copies(b, off, compact):
                        copy.wait()
                    if wide < pixels:
                        cot_rows[pl.ds(base, compact), :] = dot(
                            tables[s]["pick"][:, 0:wide], cot[b, 0:wide, :]
                        ).astype(BF)
                    else:
                        cot_rows[pl.ds(base, compact), :] = cot[b]

            @pl.when(b == 1)
            def _():
                for k in late:
                    table_copies[k].start()
                taps_copy.start()
                for each in range(images):
                    spec_copy(each).start()
                    img_copy(each).start()

        inner = jnp.minimum(b, images - 1)
        after = off + jnp.where(b < images, rows_of(inner), BLOCK - 1)
        lax.fori_loop(off // BLOCK, after // BLOCK, middle, 0)
        return after

    lax.fori_loop(0, images + 1, arrive, jnp.int32(0))
    for h in range(0, hidden, CHUNK):
        cols = slice(h, h + CHUNK)
        up_low[cols, :] = dot_t(eye[...], (0.5 * up_grad[0:width, cols]).astype(BF)).astype(BF)
        down_low[cols, :] = dot_t(eye[...], (0.5 * down_grad[:, cols]).astype(BF)).astype(BF)
    for copy in grad_copies:
        copy.start()
    for k in late:
        table_copies[k].wait()
    taps_copy.wait()

    def out_copies(b, slot):
        return (
            pltpu.make_async_copy(act_out.at[slot], act_hbm.at[b], sem_out.at[0, slot]),
            pltpu.make_async_copy(ig_out.at[slot], ig_hbm.at[b], sem_out.at[1, slot]),
        )

    def last(b, off):
        slot = lax.rem(b, 2)
        img_copy(b).wait()
        spec_copy(b).wait()

        @pl.when(b >= 2)
        def _():
            for copy in out_copies(b - 2, slot):
                copy.wait()

        for s in range(3):
            side, compact, freq, wide = shapes[s]
            table = tables[s]
            inside = lax.broadcasted_iota(jnp.int32, (extent, width), 0) < side

            @pl.when((keep[b] != 0) & group_of(b, s))
            def _():
                base = pl.multiple_of(off, 16)
                work_a[0 : 2 * freq, :] = dot(
                    table["into"][:, 0:compact], act_rows[pl.ds(base, compact), :]
                )
                for r, size in strips(freq, 48):
                    lo, hi = slice(r, r + size), slice(freq + r, freq + r + size)
                    far = slice(rows_f + r, rows_f + r + size)
                    re, im = work_a[lo, :], work_a[hi, :]
                    x_re, x_im = spectra[b, lo, :].astype(F32), spectra[b, far, :].astype(F32)
                    cross[s][lo, :] += x_re * re + x_im * im
                    cross[s][hi, :] += x_im * re - x_re * im
                    t_re, t_im = taps_f[s, lo, :], taps_f[s, far, :]
                    prod[lo, :] = (re * t_re + im * t_im).astype(BF)
                    prod[hi, :] = (im * t_re - re * t_im).astype(BF)
                work_b[0:wide, :] = dot(table["back"][:, 0 : 2 * freq], prod[0 : 2 * freq, :])
                if wide < pixels:
                    work_a[0:wide, :] = dot(
                        table["spread"][:, 0:compact], cot_rows[pl.ds(base, compact), :]
                    )
                for r, size in strips(wide, extent if wide < pixels else 48):
                    spot = slice(r, r + size)
                    arriving = cot[b, spot, :].astype(F32)
                    value = img[b, spot, :].astype(F32)
                    if wide < pixels:
                        arriving = jnp.where(inside, arriving, 0.0)
                        value = jnp.where(inside, value, 0.0)
                        branch = work_a[spot, :]
                    else:
                        branch = cot_rows[pl.ds(base + r, size), :].astype(F32)
                    ig_out[slot, spot, :] = arriving + work_b[spot, :]
                    act_out[slot, spot, :] = (value + branch).astype(BF)

            @pl.when((keep[b] == 0) & group_of(b, s))
            def _():
                for i in range(side):
                    spot = slice(i * extent, (i + 1) * extent)
                    arriving = jnp.where(inside, cot[b, spot, :].astype(F32), 0.0)
                    ig_out[slot, spot, :] = arriving
                    value = jnp.where(inside, img[b, spot, :].astype(F32), 0.0)
                    act_out[slot, spot, :] = value.astype(BF)

            if wide < pixels:

                @pl.when(group_of(b, s))
                def _():
                    ig_out[slot, wide:, :] = jnp.zeros((pixels - wide, width), F32)
                    act_out[slot, wide:, :] = jnp.zeros((pixels - wide, width), BF)

        for copy in out_copies(b, slot):
            copy.start()
        return off + rows_of(b)

    lax.fori_loop(0, images, last, jnp.int32(0))

    taps_grad = jnp.zeros((64, width), F32)
    for s in range(3):
        freq = shapes[s][2]
        whole = cross[s][...]
        high = whole.astype(BF)
        rest = (whole - high.astype(F32)).astype(BF)
        taps_hi = tables[s]["taps_hi"][:, 0 : 2 * freq]
        taps_lo = tables[s]["taps_lo"][:, 0 : 2 * freq]
        taps_grad = taps_grad + dot(taps_hi, high) + dot(taps_lo, high) + dot(taps_hi, rest)
    small[...] = taps_grad

    def total8(at):
        return jnp.sum(sums8[at : at + 8, :], axis=0, keepdims=True)

    small[49:50, :] = total8(0)
    small[50:51, :] = total8(8) * 0.5
    small[51:52, :] = total8(16) * 0.5
    small[52:53, :] = total8(24) * (scale * drop)
    small[53:54, :] = total8(32) * (0.5 * drop)
    hid = 0.5 * up_grad[width : width + 1, :]
    for k in range(hidden // width):
        small[54 + k : 55 + k, :] = hid[:, k * width : (k + 1) * width]
    for d in range(small_out.shape[0]):
        row = d * count // width
        for k in range(span):
            small_out[d, :, k * width : (k + 1) * width] = small[row + k : row + k + 1, :]
    for copy in grad_copies:
        copy.wait()
    for b in range(max(images - 2, 0), images):
        for copy in out_copies(b, b % 2):
            copy.wait()


def small_bias(rows, start, count, width):
    parts = []
    while count > 0:
        row, col = divmod(start, width)
        size = min(count, width - col)
        parts.append(rows[54 + row : 55 + row, col : col + size])
        start, count = start + size, count - size
    return parts[0] if len(parts) == 1 else jnp.concatenate(parts, axis=1)


def run_block(images, cotangent, group_ids, keep_mask, first, up_t, down, devices, small_count):
    act, normed, inv, spectra, taps, rows = first
    count, extent, _, width = images.shape
    pixels = extent * extent
    hidden = up_t.shape[0]
    span = small_span(small_count, width)
    rows_f = spectrum_rows(extent)
    groups = [make_tables(side, extent, rows_f) for side in SIDES]
    shapes = [(side, g["compact"], g["freq"], g["wide"]) for side, g in zip(SIDES, groups)]
    names, flat = [], []
    for group in groups:
        tables = {"into": low_table(group["into"]), "back": low_table(group["back"])}
        tables["taps_hi"], tables["taps_lo"] = split_table(group["taps"])
        if group["wide"] < pixels:
            tables["pick"] = low_table(group["pick"])
            tables["spread"] = low_table(group["spread"])
        names.append(tuple(tables))
        flat += [jnp.asarray(table) for table in tables.values()]
    capacity = count * pixels + BLOCK
    vmem = pl.BlockSpec(memory_space=pltpu.VMEM)
    smem = pl.BlockSpec(memory_space=pltpu.SMEM)
    hbm = pl.BlockSpec(memory_space=pltpu.HBM)
    scratch = [
        pltpu.VMEM((count, pixels, width), BF),
        pltpu.VMEM((count, pixels, width), BF),
        pltpu.VMEM((capacity, width), BF),
        pltpu.VMEM((capacity, width), BF),
        pltpu.VMEM((capacity, 128), F32),
        pltpu.VMEM((capacity, width), BF),
        pltpu.VMEM(spectra.shape, BF),
        pltpu.VMEM(taps.shape, F32),
        pltpu.VMEM((hidden, width), BF),
        pltpu.VMEM((hidden, width), BF),
        pltpu.VMEM((width, hidden), BF),
        pltpu.VMEM((width, hidden), BF),
        pltpu.VMEM((width + 16, hidden), F32),
        pltpu.VMEM((width, hidden), F32),
        pltpu.VMEM((hidden, width), BF),
        pltpu.VMEM((hidden, width), BF),
        pltpu.VMEM((2, pixels, width), BF),
        pltpu.VMEM((2, pixels, width), F32),
        pltpu.VMEM((2 * rows_f, width), F32),
        pltpu.VMEM((pixels, width), F32),
        pltpu.VMEM((2 * rows_f, width), BF),
        pltpu.VMEM((BLOCK, hidden), BF),
        pltpu.VMEM((BLOCK, hidden), BF),
        pltpu.VMEM((width + 16, BLOCK), BF),
        pltpu.VMEM((BLOCK, width), BF),
        pltpu.VMEM((width, BLOCK), BF),
        pltpu.VMEM((CHUNK, CHUNK), BF),
        pltpu.VMEM((40, width), F32),
        pltpu.VMEM((64, width), F32),
    ]
    scratch += [pltpu.VMEM(table.shape, table.dtype) for table in flat]
    scratch += [pltpu.VMEM((2 * shape[2], width), F32) for shape in shapes]
    scratch += [
        pltpu.SemaphoreType.DMA((count,)),
        pltpu.SemaphoreType.DMA((count,)),
        pltpu.SemaphoreType.DMA((3, count)),
        pltpu.SemaphoreType.DMA((count,)),
        pltpu.SemaphoreType.DMA((5,)),
        pltpu.SemaphoreType.DMA((2, 2)),
        pltpu.SemaphoreType.DMA((len(flat),)),
    ]
    work = 6 * 2 * count * pixels * width * hidden
    return pl.pallas_call(
        partial(block_kernel, shapes, names, rows_f, extent, small_count, span),
        out_shape=(
            jax.ShapeDtypeStruct((count, pixels, width), BF),
            jax.ShapeDtypeStruct((count, pixels, width), F32),
            jax.ShapeDtypeStruct((hidden, width), BF),
            jax.ShapeDtypeStruct((hidden, width), BF),
            jax.ShapeDtypeStruct((devices, 1, span * width), F32),
        ),
        in_specs=[smem, smem] + [hbm] * 9 + [vmem] + [hbm] * len(flat),
        out_specs=(hbm, hbm, hbm, hbm, vmem),
        scratch_shapes=scratch,
        compiler_params=pltpu.CompilerParams(vmem_limit_bytes=VMEM_LIMIT),
        cost_estimate=pl.CostEstimate(flops=work, bytes_accessed=30000000, transcendentals=0),
        name="block",
    )(
        group_ids,
        keep_mask,
        images.reshape(count, pixels, width),
        cotangent.reshape(count, pixels, width),
        act,
        normed,
        inv,
        spectra,
        taps,
        up_t,
        down,
        rows,
        *flat,
    )


def adam_update(weight, moment, second, grad, rate, decay):
    first = beta_one * moment + (1.0 - beta_one) * grad
    second_new = beta_two * second + (1.0 - beta_two) * grad * grad
    step_dir = (
        first / (1.0 - beta_one**STEP) / (jnp.sqrt(second_new / (1.0 - beta_two**STEP)) + adam_eps)
    )
    return (weight - rate * (step_dir + decay * weight), first, second_new)


def wide_split(wide):
    chips = wide // 2
    high = 1
    while high * high < chips:
        high *= 2
    return high, chips // high


AXES = "hlcn"
GATHER_ROUTES = ("nhl", "lnh", "hln")
SCATTER_ROUTES = ("lhn", "hnl", "nlh")


class Place:
    def __init__(self, wide, narrow):
        high, low = wide_split(wide)
        self.sizes = dict(h=high, l=low, c=2, n=narrow)
        spot = lax.axis_index("wide")
        self.at = dict(
            h=spot // (2 * low),
            l=lax.rem(spot // 2, low),
            c=lax.rem(spot, 2),
            n=lax.axis_index("narrow"),
        )

    def shifted(self, axis, step):
        return lax.rem(self.at[axis] + step, self.sizes[axis])

    def device(self, axis, step):
        at = dict(self.at)
        at[axis] = self.shifted(axis, step)
        wide = (at["h"] * self.sizes["l"] + at["l"]) * 2 + at["c"]
        return {"wide": wide, "narrow": at["n"]}

    def peers(self):
        return [(axis, k) for axis in AXES for k in range(1, self.sizes[axis])]

    def greet(self):
        for axis, k in self.peers():
            pl.semaphore_signal(
                pltpu.get_barrier_semaphore(),
                inc=1,
                device_id=self.device(axis, k),
                device_id_type=pl.DeviceIdType.MESH,
            )

    def met(self):
        pl.semaphore_wait(pltpu.get_barrier_semaphore(), len(self.peers()))


def send(src, dst, sems, number, device):
    copy = pltpu.make_async_remote_copy(
        src_ref=src,
        dst_ref=dst,
        send_sem=sems[0].at[number],
        recv_sem=sems[1].at[number],
        device_id=device,
        device_id_type=pl.DeviceIdType.MESH,
    )
    copy.start()
    return copy


def make_parts(spaced, routes):
    tiles = spaced // 16
    cut = 16 * ((2 * tiles + 2) // 3)
    parts = [(2, (0, 1), routes[1]), (0, (0, spaced), routes[0]), (1, (0, cut), routes[1])]
    if cut < spaced:
        parts.append((1, (cut, spaced), routes[2]))
    return parts


def in_order(count, phases):
    return [(p, phase) for phase in range(phases) for p in range(count)]


def gather_copies(sizes):
    count = 1
    for axis in "hln":
        count += 2 * (sizes[axis] - 1)
    return count


def small_span(count, width):
    return (width + count - 2) // width + 1


def small_shift(wide, narrow, count, width):
    device = lax.axis_index("wide") * narrow + lax.axis_index("narrow")
    return lax.rem(device * count, width)


def gather_kernel(wide, narrow, parts, rows_f, *refs):
    refs = list(refs)

    def take(number):
        got = refs[:number]
        del refs[:number]
        return got

    gid = take(1)[0]
    far, img_hbm, far_tables = take(3), take(1)[0], take(3)
    up_hbm, down_hbm, rows, far_first = take(2) + [take(1)[0], take(5)]
    near, tables, bufs = take(3), take(3), take(3)
    img, xhat, act, normed, inv, spectra, taps_f = take(7)
    work, prod, rows_low, small_row = take(4)
    sem_in, sem_img, sem_tables, sem_first, sem_mats, send_sem, recv_sem = take(7)
    into, back, taps_in = tables
    place = Place(wide, narrow)
    here = tuple(place.at[axis] for axis in AXES)
    images, pixels, width = img.shape
    place.greet()
    fetch = [pltpu.make_async_copy(far[w], near[w], sem_in.at[w]) for w in range(3)]
    for copy in fetch:
        copy.start()
    fetch_tables = [
        pltpu.make_async_copy(far_tables[k], tables[k], sem_tables.at[k]) for k in range(3)
    ]

    def img_copy(b):
        return pltpu.make_async_copy(img_hbm.at[b], img.at[b], sem_img.at[b])

    for copy in fetch:
        copy.wait()
    fetch_tables[0].start()
    for b in range(images):
        img_copy(b).start()
    for copy in fetch_tables[1:]:
        copy.start()
    own, count = near[0].shape[0], near[2].shape[0]
    spaced = bufs[0].shape[4]
    for w in range(2):
        if own < spaced:
            bufs[w][here] = jnp.zeros(bufs[w].shape[4:], BF)
        bufs[w][here + (slice(0, own),)] = near[w][...].astype(BF)
    small_row[...] = jnp.zeros_like(small_row)
    small_row[:, 0:count] = near[2][...].reshape(1, count).astype(BF).astype(F32)
    bufs[2][here] = pltpu.roll(small_row[...], small_shift(wide, narrow, count, width), 1)
    place.met()
    sems = (send_sem, recv_sem)
    have = [dict(place.at) for _ in parts]
    started, sibling = [], []
    waiting = [None] * len(parts)
    passed = [[] for _ in parts]

    def region(p):
        which, bounds, _ = parts[p]
        return bufs[which].at[tuple(have[p][axis] for axis in AXES) + (slice(*bounds),)]

    def send_phase(p, phase):
        which, bounds, route = parts[p]
        axis = route[phase]
        waiting[p] = []
        for k in range(1, place.sizes[axis]):
            part = region(p)
            number = len(started) + len(sibling)
            waiting[p].append(send(part, part, sems, number, place.device(axis, k)))
            started.append(waiting[p][-1])

    def pass_over(p):
        number = len(started) + len(sibling)
        part = region(p)
        copy = send(part, part, sems, number, place.device("c", 1))
        sibling.append(copy)
        passed[p].append(copy)

    def finish_phase(p, phase):
        axis = parts[p][2][phase]
        for copy in waiting[p]:
            copy.wait_recv()
        before = have[p]
        have[p] = dict(before)
        have[p][axis] = slice(None)
        after = have[p]
        if phase < 2:
            send_phase(p, phase + 1)
        if phase == 0:
            pass_over(p)
        else:
            for k in range(1, place.sizes[axis]):
                have[p] = dict(before)
                have[p][axis] = place.shifted(axis, k)
                pass_over(p)
            have[p] = after

    def spectrum(b, carry):
        img_copy(b).wait()
        value = dot(into[gid[b], :, 0:pixels], img[b])
        xhat[b] = value
        spectra[b] = value.astype(BF)
        return carry

    def first_copies(b):
        pairs = zip((act, normed, inv, spectra), far_first)
        return [
            pltpu.make_async_copy(close.at[b], away.at[b], sem_first.at[k, b])
            for k, (close, away) in enumerate(pairs)
        ]

    def convolve(b, carry):
        g = gid[b]
        for r, size in strips(rows_f, 48):
            lo, hi = slice(r, r + size), slice(rows_f + r, rows_f + r + size)
            re, im = xhat[b, lo, :], xhat[b, hi, :]
            t_re, t_im = taps_f[g, lo, :], taps_f[g, hi, :]
            prod[lo, :] = (re * t_re - im * t_im).astype(BF)
            prod[hi, :] = (re * t_im + im * t_re).astype(BF)
        work[...] = dot(back[g, :, 0 : 2 * rows_f], prod[...])
        conv_bias, gain, norm_bias = rows[49:50, :], rows[50:51, :], rows[51:52, :]
        for r, size in strips(pixels, 64):
            span = slice(r, r + size)
            conv = work[span, :] + conv_bias
            center = conv - jnp.mean(conv, axis=1, keepdims=True)
            scale = lax.rsqrt(jnp.mean(center * center, axis=1, keepdims=True) + 1e-06)
            value = center * scale
            normed[b, span, :] = value.astype(BF)
            inv[b, span, :] = jnp.broadcast_to(scale, (size, 128))
            act[b, span, :] = (value * gain + norm_bias).astype(BF)
        for copy in first_copies(b):
            copy.start()
        return carry

    big = range(1, len(parts))
    ahead = max(images - 3, 0)
    for p in range(len(parts)):
        send_phase(p, 0)
    fetch_tables[0].wait()
    lax.fori_loop(0, images // 4, spectrum, 0)
    for p in range(len(parts)):
        finish_phase(p, 0)
    lax.fori_loop(images // 4, images // 2, spectrum, 0)
    finish_phase(0, 1)
    lax.fori_loop(images // 2, 3 * images // 4, spectrum, 0)
    finish_phase(0, 2)
    lax.fori_loop(3 * images // 4, images, spectrum, 0)
    for p in big:
        finish_phase(p, 1)
    for copy in fetch_tables[1:]:
        copy.wait()
    for copy in passed[0]:
        copy.wait_recv()
    collect_rows(bufs[2], count, rows)
    rows_low[0:64, :] = rows[...].astype(BF)
    rows_low[64:128, :] = rows[...].astype(BF)
    for s in range(3):
        taps_f[s] = dot(taps_in[s], rows_low[...])
    taps_copy = pltpu.make_async_copy(taps_f, far_first[4], sem_mats.at[2])
    taps_copy.start()
    lax.fori_loop(0, ahead, convolve, 0)
    for p in big:
        finish_phase(p, 2)
    lax.fori_loop(ahead, images - 1, convolve, 0)
    for p in big:
        for copy in passed[p]:
            copy.wait_recv()
    mats = [
        pltpu.make_async_copy(bufs[0], up_hbm, sem_mats.at[0]),
        pltpu.make_async_copy(bufs[1], down_hbm, sem_mats.at[1]),
    ]
    for copy in mats:
        copy.start()
    lax.fori_loop(images - 1, images, convolve, 0)

    def settle(b, carry):
        for copy in first_copies(b):
            copy.wait()
        return carry

    lax.fori_loop(0, images, settle, 0)
    for copy in mats:
        copy.wait()
    taps_copy.wait()
    for copy in started + sibling:
        copy.wait_send()


def collect_rows(pieces, count, rows):
    high, low, cores, narrow = pieces.shape[:4]
    width = rows.shape[1]
    terms = [[] for _ in range(rows.shape[0])]
    for d in range(high * low * cores * narrow):
        spot = (d // (low * cores * narrow), d // (cores * narrow) % low, d // narrow % cores, d % narrow)
        first, final = d * count // width, (d * count + count - 1) // width
        for r in range(first, final + 1):
            terms[r].append(pieces[spot][:, (r - first) * width : (r - first + 1) * width])
    for r, parts in enumerate(terms):
        value = jnp.zeros((1, width), F32)
        for part in parts:
            value = value + part
        rows[r : r + 1, :] = value


def gather_weights(wide, narrow, weights, images, group_ids):
    up, down, small = weights
    high, low = wide_split(wide)
    sizes = dict(h=high, l=low, n=narrow)
    own, width = up.shape
    images_n, extent = images.shape[:2]
    pixels = extent * extent
    count = small.shape[0]
    spaced = round_up(own, 16)
    lanes = small_span(count, width) * width
    grid = (high, low, 2, narrow)
    rows_f = spectrum_rows(extent)
    hbm = pl.BlockSpec(memory_space=pltpu.HBM)
    smem = pl.BlockSpec(memory_space=pltpu.SMEM)
    parts = make_parts(spaced, GATHER_ROUTES)
    copies = len(parts) * gather_copies(sizes)
    groups = [make_tables(side, extent, rows_f) for side in SIDES]
    tables = [
        low_table(np.stack([g["first_into"] for g in groups])),
        low_table(np.stack([g["first_back"] for g in groups])),
        stacked_split(np.stack([g["first_taps"] for g in groups])),
    ]
    first = [
        jax.ShapeDtypeStruct((images_n, pixels, width), BF),
        jax.ShapeDtypeStruct((images_n, pixels, width), BF),
        jax.ShapeDtypeStruct((images_n, pixels, 128), F32),
        jax.ShapeDtypeStruct((images_n, 2 * rows_f, width), BF),
        jax.ShapeDtypeStruct((3, 2 * rows_f, width), F32),
    ]
    bufs = [
        jax.ShapeDtypeStruct(grid + (spaced, width), BF),
        jax.ShapeDtypeStruct(grid + (spaced, width), BF),
        jax.ShapeDtypeStruct(grid + (1, lanes), F32),
    ]
    near = [
        pltpu.VMEM((own, width), F32),
        pltpu.VMEM((own, width), F32),
        pltpu.VMEM((count,), F32),
    ]
    scratch = near + [pltpu.VMEM(table.shape, BF) for table in tables]
    scratch += [pltpu.VMEM(buf.shape, buf.dtype) for buf in bufs]
    scratch += [
        pltpu.VMEM((images_n, pixels, width), BF),
        pltpu.VMEM((images_n, 2 * rows_f, width), F32),
    ]
    scratch += [pltpu.VMEM(part.shape, part.dtype) for part in first]
    scratch += [
        pltpu.VMEM((pixels, width), F32),
        pltpu.VMEM((2 * rows_f, width), BF),
        pltpu.VMEM((128, width), BF),
        pltpu.VMEM((1, lanes), F32),
        pltpu.SemaphoreType.DMA((3,)),
        pltpu.SemaphoreType.DMA((images_n,)),
        pltpu.SemaphoreType.DMA((4,)),
        pltpu.SemaphoreType.DMA((4, images_n)),
        pltpu.SemaphoreType.DMA((3,)),
        pltpu.SemaphoreType.DMA((copies,)),
        pltpu.SemaphoreType.DMA((copies,)),
    ]
    out = pl.pallas_call(
        partial(gather_kernel, wide, narrow, parts, rows_f),
        out_shape=tuple(bufs[:2] + [jax.ShapeDtypeStruct((64, width), F32)] + first),
        in_specs=[smem] + [hbm] * 7,
        out_specs=(hbm, hbm, pl.BlockSpec(memory_space=pltpu.VMEM)) + (hbm,) * 5,
        scratch_shapes=scratch,
        compiler_params=pltpu.CompilerParams(
            collective_id=0, has_side_effects=True, vmem_limit_bytes=VMEM_LIMIT
        ),
        name="gather",
    )(
        group_ids,
        up,
        down,
        small,
        images.reshape(images_n, pixels, width),
        *[jnp.asarray(table) for table in tables],
    )
    return out[0], out[1], out[3:] + (out[2],)


def scatter_shapes(sizes, parts, spaced, width, lanes):
    shapes = []
    for which, bounds, route in parts:
        tail, dtype = ((bounds[1] - bounds[0], width), BF) if which < 2 else ((1, lanes), F32)
        left = dict(h=sizes["h"], l=sizes["l"], n=sizes["n"])
        shapes.append(pltpu.VMEM(tuple(left.values()) + tail, dtype))
        for axis in route:
            del left[axis]
            shapes.append(
                pltpu.VMEM((max(sizes[axis] - 1, 1),) + tuple(left.values()) + tail, dtype)
            )
    return shapes


def scatter_kernel(wide, narrow, parts, *refs):
    refs = list(refs)

    def take(count):
        got = refs[:count]
        del refs[:count]
        return got

    far = take(3)
    sums_out = take(3)
    own, sums = take(3), take(3)
    landing = [take(4) for _ in parts]
    sem_own, send_sem, recv_sem = take(3)
    sems = (send_sem, recv_sem)
    place = Place(wide, narrow)
    place.greet()
    at, sizes = place.at, place.sizes
    full = slice(None)
    fetch = [
        pltpu.make_async_copy(far[w].at[full, full, at["c"]], own[w], sem_own.at[w])
        for w in range(3)
    ]
    for copy in fetch:
        copy.start()
    place.met()
    started = []
    for p, (which, bounds, route) in enumerate(parts):
        src = far[which].at[full, full, 1 - at["c"], full, slice(*bounds)]
        started.append(send(src, landing[p][0], sems, len(started), place.device("c", 1)))
    waiting = [[copy] for copy in started]
    left = [dict(h=full, l=full, n=full) for _ in parts]

    def spot(fixed):
        return tuple(fixed[axis] for axis in "hln")

    def send_phase(p, phase):
        which, bounds, route = parts[p]
        axis = route[phase]
        waiting[p] = []
        for k in range(1, sizes[axis]):
            there = dict(left[p])
            there[axis] = place.shifted(axis, k)
            src = sums[which].at[spot(there) + (slice(*bounds),)]
            dst = landing[p][1 + phase].at[k - 1]
            copy = send(src, dst, sems, len(started), place.device(axis, k))
            waiting[p].append(copy)
            started.append(copy)

    for copy in fetch:
        copy.wait()
    for p, phase in in_order(len(parts), 4):
        which, bounds, route = parts[p]
        rows = slice(*bounds)
        for copy in waiting[p]:
            copy.wait_recv()
        if phase == 0:
            for h in range(sizes["h"]):
                for l in range(sizes["l"]):
                    both = own[which][h, l, :, rows].astype(F32) + landing[p][0][h, l].astype(F32)
                    sums[which][h, l, :, rows] = both.astype(sums[which].dtype)
            send_phase(p, 0)
            continue
        axis = route[phase - 1]
        left[p][axis] = at[axis]
        target = spot(left[p]) + (rows,)
        total = sums[which][target].astype(F32)
        for k in range(1, sizes[axis]):
            total = total + landing[p][phase][k - 1].astype(F32)
        if phase < 3:
            sums[which][target] = total.astype(sums[which].dtype)
            send_phase(p, phase)
        else:
            sums_out[which][rows] = total
    for copy in started:
        copy.wait_send()


def scatter_sums(wide, narrow, partials):
    high, low = wide_split(wide)
    sizes = dict(h=high, l=low, n=narrow)
    spaced, width = partials[0].shape[4:]
    lanes = partials[2].shape[5]
    parts = make_parts(spaced, SCATTER_ROUTES)
    copies = len(parts) * (1 + sum(sizes[axis] - 1 for axis in "hln"))
    hbm = pl.BlockSpec(memory_space=pltpu.HBM)
    vmem = pl.BlockSpec(memory_space=pltpu.VMEM)
    grid = (high, low, narrow)
    halves = [
        pltpu.VMEM(grid + (spaced, width), BF),
        pltpu.VMEM(grid + (spaced, width), BF),
        pltpu.VMEM(grid + (1, lanes), F32),
    ]
    scratch = halves + halves + scatter_shapes(sizes, parts, spaced, width, lanes)
    scratch += [
        pltpu.SemaphoreType.DMA((3,)),
        pltpu.SemaphoreType.DMA((copies,)),
        pltpu.SemaphoreType.DMA((copies,)),
    ]
    return pl.pallas_call(
        partial(scatter_kernel, wide, narrow, parts),
        out_shape=(
            jax.ShapeDtypeStruct((spaced, width), F32),
            jax.ShapeDtypeStruct((spaced, width), F32),
            jax.ShapeDtypeStruct((1, lanes), F32),
        ),
        in_specs=[hbm] * 3,
        out_specs=(vmem,) * 3,
        scratch_shapes=scratch,
        compiler_params=pltpu.CompilerParams(
            collective_id=1, has_side_effects=True, vmem_limit_bytes=VMEM_LIMIT
        ),
        name="scatter",
    )(*partials)


def update_kernel(wide, narrow, width, *refs):
    grads, weights, moments, seconds = refs[0:3], refs[3:6], refs[6:9], refs[9:12]
    news, firsts, nexts, lows = refs[12:15], refs[15:18], refs[18:21], refs[21:24]
    for which in range(3):
        shape = weights[which].shape
        if which < 2:
            grad = grads[which][0 : shape[0], :]
        else:
            lanes = grads[which].shape[1]
            shift = lanes - small_shift(wide, narrow, shape[0], width)
            grad = pltpu.roll(grads[which][...], shift, 1)[:, 0 : shape[0]]

        def flat(value):
            return value if which < 2 else value.reshape(1, shape[0])

        rate, decay = (rate_mats, decay_mats) if which < 2 else (rate_small, 0.0)
        new, first, second = adam_update(
            flat(weights[which][...]),
            flat(moments[which][...]),
            flat(seconds[which][...]),
            grad,
            rate,
            decay,
        )
        news[which][...] = new.reshape(shape)
        firsts[which][...] = first.reshape(shape)
        nexts[which][...] = second.reshape(shape)
        lows[which][...] = new.reshape(shape).astype(BF)


def update(wide, narrow, grads, weights, moments, seconds):
    like = [jax.ShapeDtypeStruct(weight.shape, F32) for weight in weights]
    low = [jax.ShapeDtypeStruct(weight.shape, BF) for weight in weights]
    vmem = pl.BlockSpec(memory_space=pltpu.VMEM)
    return pl.pallas_call(
        partial(update_kernel, wide, narrow, weights[0].shape[1]),
        out_shape=tuple(like * 3 + low),
        in_specs=[vmem] * 12,
        out_specs=(vmem,) * 12,
        compiler_params=pltpu.CompilerParams(vmem_limit_bytes=VMEM_LIMIT),
        name="update",
    )(*grads, *weights, *moments, *seconds)


def per_device(
    wide,
    narrow,
    images,
    cotangent,
    group_ids,
    keep_mask,
    up_weight,
    down_weight,
    small_params,
    up_moment,
    down_moment,
    small_moment,
    up_second,
    down_second,
    small_second,
):
    width = images.shape[3]
    own, count = down_weight.shape[0], small_params.shape[0]
    devices = wide * narrow

    def laid(three):
        return three[0].T, three[1], three[2]

    weights = laid((up_weight, down_weight, small_params))
    moments = laid((up_moment, down_moment, small_moment))
    seconds = laid((up_second, down_second, small_second))
    gu, gd, first = gather_weights(wide, narrow, weights, images, group_ids)
    grid, spaced = gu.shape[:4], gu.shape[4]

    def dense(blocks):
        return blocks.reshape(devices, spaced, width)[:, :own].reshape(devices * own, width)

    def spread(rows):
        rows = rows.reshape(devices, own, width)
        return jnp.pad(rows, ((0, 0), (0, spaced - own), (0, 0))).reshape(
            grid + (spaced, width)
        )

    activations, input_grad, up_part, down_part, small_part = run_block(
        images, cotangent, group_ids, keep_mask, first, dense(gu), dense(gd), devices, count
    )
    small_part = small_part.reshape(grid + small_part.shape[1:])
    grads = scatter_sums(wide, narrow, (spread(up_part), spread(down_part), small_part))
    out = update(wide, narrow, grads, weights, moments, seconds)
    groups = [(out[k].T, out[k + 1], out[k + 2]) for k in range(0, 12, 3)]
    maps = (activations.reshape(images.shape), input_grad.reshape(images.shape))
    return maps + groups[0] + groups[1] + groups[2] + groups[3]


def solution(mesh):
    both = ("wide", "narrow")
    maps = P(both, None, None, None)
    cols, rows, flat = P(None, both), P(both, None), P(both)
    three = (cols, rows, flat)
    return jax.shard_map(
        partial(per_device, mesh.shape["wide"], mesh.shape["narrow"]),
        mesh=mesh,
        in_specs=(maps, maps, flat, flat) + three * 3,
        out_specs=(maps, maps) + three * 4,
        check_vma=False,
    )
```
